256 devices in a mesh: samp: 64 (over z, y_hi, x), band: 4 (over y_lo, core).
Axes of the slice: x: 4, y: 4 (y_hi: 2, y_lo: 2; y = y_hi * 2 + y_lo), z: 8, core: 2. Of those that a mesh axis runs over, the one named last changes fastest.
Arguments:
- features: bfloat16 [16384, 1024], P('samp', 'band'), may hold values from -6 to 6
- direction: bfloat16 [16384, 256], P('samp'), may hold values from -6 to 6
- cotangent: bfloat16 [16384, 256], P('samp'), may hold values from -6 to 6
- residual: float32 [16384, 256], P('samp', 'band'), may hold values from -6 to 6
- band_logw: float32 [4], P('band'), may hold values from -1 to 1
- ridge: float32 [1], replicated, may hold values from 0.5 to 2
Outputs:
- residual_next: float32 [16384, 256], P('samp', 'band')
- adjoint: float32 [16384, 256], P('samp', 'band')
- band_grad: float32 [4], P('band')
The draws below stay inside these ranges and needn't reach their ends.
All inputs are finite; a program needn't handle non-finite values.
Results may differ from the reference program's by a relative error of at most 0.0018.
The reference program's roundings to bfloat16 on the way count: a program that leaves them out, or rounds other values in their place, can miss the bound.
Values may be sent and summed in bfloat16 or wider, within the bound.
No kernel may reach another device: no remote copies, remote signals or barrier semaphores. Data moves between devices by JAX's collectives and lax.ppermute only.
A program may use at most 128 MiB of HBM per device.

```python
import math
import jax
import jax.numpy as jnp
from jax import lax

F = 256
V = 256
BANDS = 4
ROWS = 256
NTOT = 16384


def block_levels(rng, dims, split, least, largest):
    loudness = 1.0
    for position, parts in split:
        heights = jax.random.uniform(jax.random.fold_in(jax.random.fold_in(rng, 6), position), (parts,), jnp.float32, least / len(split), largest / len(split))
        loudness = loudness * jnp.repeat(jnp.exp(heights), dims[position] // parts).reshape((-1,) + (1,) * (len(dims) - 1 - position))
    return loudness


def noise(stream_key, dims, spread, limit, pieces=(), dtype=jnp.bfloat16):
    result = jax.random.normal(stream_key, dims, jnp.float32) * spread
    if len(pieces) > 0:
        result = block_levels(stream_key, dims, pieces, -0.22, 0.18) * result
    return jnp.clip(result, min=-limit, max=limit).astype(dtype)


def setup_inputs(seed: int = 0) -> dict:
    seeds = jax.random.split(jax.random.key(seed), 7)
    features = noise(seeds[0], (NTOT, BANDS * F), 1.0, 6.0, ((0, 64), (1, 4)))
    direction = noise(seeds[1], (NTOT, V), 1.0, 6.0, ((0, 64),))
    cotangent = noise(seeds[2], (NTOT, V), 1.0, 6.0, ((0, 64),))
    residual = noise(seeds[3], (NTOT, V), 1.0, 6.0, ((0, 64), (1, 4)), jnp.float32)
    band_logw = jnp.clip(jax.random.uniform(seeds[4], (BANDS,), jnp.float32, -1.0, 1.0) * block_levels(seeds[4], (BANDS,), ((0, 4),), -0.4, 0.0), -1.0, 1.0)
    ridge = jnp.clip(jnp.exp(jax.random.uniform(seeds[5], (1,), jnp.float32, math.log(0.5), math.log(2.0))), 0.5, 2.0)
    return {"features": features, "direction": direction, "cotangent": cotangent, "residual": residual, "band_logw": band_logw, "ridge": ridge}


def reference(features, direction, cotangent, residual, band_logw, ridge):
    total = features.shape[0]
    weights = jnp.exp(band_logw) * (1.0 / math.sqrt(total))
    inv_root = 1.0 / math.sqrt(F)
    count = total // ROWS
    cot_full = cotangent.astype(jnp.float32)

    def one_block(start):
        block_feat = lax.dynamic_slice_in_dim(features, start, ROWS, 0)
        block_cot = lax.dynamic_slice_in_dim(cot_full, start, ROWS, 0)
        prod_sum = jnp.zeros((ROWS, V), jnp.float32)
        adj_sum = jnp.zeros((ROWS, V), jnp.float32)
        grads = []
        for band in range(BANDS):
            rows_b = block_feat[:, band * F:(band + 1) * F]
            all_b = features[:, band * F:(band + 1) * F]
            inner = jnp.einsum('rf,cf->rc', rows_b, all_b, preferred_element_type=jnp.float32) * inv_root
            tile = ((inner + 1.0) ** 2).astype(jnp.bfloat16)
            kp = jnp.dot(tile, direction, preferred_element_type=jnp.float32)
            kg = jnp.dot(tile, cotangent, preferred_element_type=jnp.float32)
            prod_sum = prod_sum + weights[band] * kp
            adj_sum = adj_sum + weights[band] * kg
            grads.append(weights[band] * jnp.sum(block_cot * kp))
        return (prod_sum, adj_sum, jnp.stack(grads))
    starts = (jnp.arange(count) * ROWS).astype(jnp.int32)
    prod_blocks, adj_blocks, grad_blocks = lax.map(one_block, starts)
    product = prod_blocks.reshape(total, V) + ridge[0] * direction.astype(jnp.float32)
    adjoint = adj_blocks.reshape(total, V) + ridge[0] * cot_full
    band_grad = lax.optimization_barrier(jnp.sum(grad_blocks, axis=0))
    squares = lax.optimization_barrier(jnp.sum(residual * residual, axis=0))
    curvature = lax.optimization_barrier(jnp.sum(direction.astype(jnp.float32) * product, axis=0))
    residual_next = residual - squares / curvature * product
    return (residual_next, adjoint, band_grad)
```

```python
import math

import jax
import jax.numpy as jnp
from jax import lax
from jax.experimental import pallas as pl
from jax.experimental.pallas import tpu as pltpu
from jax.sharding import Mesh, PartitionSpec as P

SIZES = {"z": 8, "yh": 2, "x": 4, "yl": 2, "core": 2}
SAMP = ("z", "yh", "x")
BAND = ("yl", "core")
ZD = (0, -1, 1, -2, 2, -3, 3, 4)
XD = (0, -1, 1, 2)


def send(value, axis, step):
    n = SIZES[axis]
    return lax.ppermute(value, axis, [(i, (i + step) % n) for i in range(n)])


def pair_kernel(w_ref, *refs):
    zs, zo, ps, po = refs[0:9], refs[9:18], refs[18:26], refs[26:34]
    pm_ref, pq_ref, gm_ref, gq_ref, bg_ref = refs[34:39]
    xr, xc, dd, ct, acc = refs[39:]
    for i in range(8):
        if i < 7:
            xc[i] = zs[i][:, 0:256]
            dd[i, :, 0:128] = zs[i][:, 256:384]
            dd[i, :, 128:256] = zo[i][:, 256:384]
        else:
            for h in range(2):
                rows = slice(128 * h, 128 * h + 128)
                xc[i, rows, :] = zs[i + h][:, 0:256]
                dd[i, rows, 0:128] = zs[i + h][:, 256:384]
                dd[i, rows, 128:256] = zo[i + h][:, 256:384]
        cols = slice(256 * i, 256 * i + 256)
        xr[cols, :] = ps[i][0:256, :] * jnp.bfloat16(0.0625)
        ct[0:128, cols] = ps[i][256:384, :]
        ct[128:256, cols] = po[i][256:384, :]
    acc[...] = jnp.zeros_like(acc)
    w = w_ref[0]

    def column(j, carry):
        x_c = xc[j]
        d_c = dd[j]
        total = jnp.zeros((256, 256), jnp.float32)
        for h in range(2):
            rows = slice(1024 * h, 1024 * h + 1024)
            inner = lax.dot_general(
                xr[rows, :], x_c, (((1,), (1,)), ((), ())), preferred_element_type=jnp.float32
            )
            inner = inner + 1.0
            tile = (inner * inner).astype(jnp.bfloat16)
            acc[rows, :] += jnp.dot(tile, d_c, preferred_element_type=jnp.float32)
            total += jnp.dot(ct[:, rows], tile, preferred_element_type=jnp.float32)
        total = total * w
        gm_ref[j] = total[0:128, :]
        gq_ref[j] = total[128:256, :]
        return carry

    lax.fori_loop(0, 8, column, 0)
    grad = jnp.zeros((256, 256), jnp.float32)
    for i in range(8):
        cols = slice(256 * i, 256 * i + 256)
        part = acc[cols, :] * w
        pm_ref[i] = part[:, 0:128]
        pq_ref[i] = part[:, 128:256]
        grad += part * ct[:, cols].astype(jnp.float32).T
    bg_ref[...] = jnp.sum(grad.reshape(32, 8, 2, 128), axis=(0, 2))


def pairs(weight, zs, zo, ps, po):
    f32 = jnp.float32
    bf16 = jnp.bfloat16
    return pl.pallas_call(
        pair_kernel,
        out_shape=(
            jax.ShapeDtypeStruct((8, 256, 128), f32),
            jax.ShapeDtypeStruct((8, 256, 128), f32),
            jax.ShapeDtypeStruct((8, 128, 256), f32),
            jax.ShapeDtypeStruct((8, 128, 256), f32),
            jax.ShapeDtypeStruct((8, 128), f32),
        ),
        in_specs=[pl.BlockSpec(memory_space=pltpu.SMEM)]
        + [pl.BlockSpec(memory_space=pltpu.VMEM)] * 34,
        out_specs=(pl.BlockSpec(memory_space=pltpu.VMEM),) * 5,
        scratch_shapes=[
            pltpu.VMEM((2048, 256), bf16),
            pltpu.VMEM((8, 256, 256), bf16),
            pltpu.VMEM((8, 256, 256), bf16),
            pltpu.VMEM((256, 2048), bf16),
            pltpu.VMEM((2048, 256), f32),
        ],
        compiler_params=pltpu.CompilerParams(vmem_limit_bytes=48 * 1024 * 1024),
        name="pairs",
    )(weight, *zs, *zo, *ps, *po)


def voxel_chunk(array, chunk, axis):
    return lax.dynamic_slice_in_dim(array, chunk * 64, 64, axis)


def body(features, direction, cotangent, residual, band_logw, ridge):
    f32 = jnp.float32
    total = features.shape[0] * 64
    weight = jnp.exp(band_logw) * (1.0 / math.sqrt(total))
    yl = lax.axis_index("yl")
    core = lax.axis_index("core")
    own = 2 * yl + core
    also = 2 * (1 - yl) + core

    z0 = jnp.concatenate(
        [features, voxel_chunk(direction, own, 1), voxel_chunk(direction, also, 1)], axis=1
    )
    cot_t = cotangent.T
    p0 = jnp.concatenate(
        [features, voxel_chunk(cot_t, own, 0), voxel_chunk(cot_t, also, 0)], axis=0
    )
    f1, b1 = send(z0, "z", 1), send(z0, "z", -1)
    p_f1, p_b1, q0 = send(p0, "x", 1), send(p0, "x", -1), send(p0, "yh", 1)
    f2, b2 = send(f1, "z", 1), send(b1, "z", -1)
    q_f1, q_b1 = send(q0, "x", 1), send(q0, "x", -1)
    f3, b3 = send(f2, "z", 1), send(b2, "z", -1)
    p2, q2 = send(p_f1, "x", 1), send(q_b1, "x", -1)
    f4, b4 = send(f3[0:128], "z", 1), send(b3[128:256], "z", -1)
    zs = (z0, f1, b1, f2, b2, f3, b3, f4, b4)
    ps = (p0, p_f1, p_b1, p2, q0, q_f1, q_b1, q2)
    zo = tuple(send(v, "core", 1) for v in zs)
    po = tuple(send(v, "core", 1) for v in ps)

    p_mine, p_other, g_mine, g_other, grad = pairs(weight, zs, zo, ps, po)
    p_core = send(p_other, "core", 1)
    g_core = send(g_other, "core", 1)

    pb = {}
    for y in range(2):
        for i, d in enumerate(XD):
            pb[y, d] = p_mine[4 * y + i] + p_core[4 * y + i]
    far_f = send(pb[0, 2], "x", 1)
    far_b = send(pb[1, 2], "x", -1)
    near_f = send(jnp.concatenate([pb[0, 1] + far_f, pb[1, 1]]), "x", 1)
    near_b = send(jnp.concatenate([pb[0, -1], pb[1, -1] + far_b]), "x", -1)
    across = send(pb[1, 0] + near_f[256:] + near_b[256:], "yh", 1)
    mine = pb[0, 0] + near_f[:256] + near_b[:256] + across
    product = mine[:, 0:64] + send(mine[:, 64:128], "yl", 1)

    gb = {d: g_mine[i] + g_core[i] for i, d in enumerate(ZD)}
    gf = send(gb[4][0:64], "z", 1)
    gr = send(gb[4][64:128], "z", -1)
    gf = send(jnp.concatenate([gb[3][0:64] + gf, gb[3][64:128]]), "z", 1)
    gr = send(jnp.concatenate([gb[-3][0:64], gb[-3][64:128] + gr]), "z", -1)
    gf = send(gb[2] + gf, "z", 1)
    gr = send(gb[-2] + gr, "z", -1)
    gf = send(gb[1] + gf, "z", 1)
    gr = send(gb[-1] + gr, "z", -1)
    adj = gb[0] + gf + gr
    adj = adj[0:64] + send(adj[64:128], "yl", 1)
    adjoint = adj.T + ridge[0] * voxel_chunk(cotangent, own, 1).astype(f32)

    dir_own = voxel_chunk(direction, own, 1).astype(f32)
    product = product + ridge[0] * dir_own
    sums = jnp.concatenate(
        [
            jnp.sum(residual * residual, axis=0),
            jnp.sum(dir_own * product, axis=0),
            jnp.sum(grad, axis=0),
        ]
    ).reshape(1, 256)
    sums = sums + sum(send(sums, "z", k) for k in range(1, 8))
    half = sum(send(sums, "x", k) for k in range(1, 4)) + sums
    sums = half + send(half, "yh", 1)
    residual_next = residual - sums[:, 0:64] / sums[:, 64:128] * product
    return (residual_next, adjoint, jnp.sum(sums[0, 128:256]).reshape(1))


def solution(mesh):
    parts = Mesh(mesh.devices.reshape(tuple(SIZES.values())), tuple(SIZES))
    placed = (P(SAMP, BAND), P(SAMP), P(SAMP), P(SAMP, BAND), P(BAND), P())
    return jax.shard_map(
        body,
        mesh=parts,
        in_specs=placed,
        out_specs=(P(SAMP, BAND), P(SAMP, BAND), P(BAND)),
        check_vma=False,
    )
```

```python
import math

import jax
import jax.numpy as jnp
from jax import lax
from jax.experimental import pallas as pl
from jax.experimental.pallas import tpu as pltpu
from jax.sharding import Mesh, PartitionSpec as P

SIZES = {"z": 8, "yh": 2, "x": 4, "yl": 2, "core": 2}
SAMP = ("z", "yh", "x")
BAND = ("yl", "core")
F32 = jnp.float32
BF16 = jnp.bfloat16
NT = (((1,), (1,)), ((), ()))


def send(value, axis, step):
    n = SIZES[axis]
    return lax.ppermute(value, axis, [(i, (i + step) % n) for i in range(n)])


def load_rows(xr, ct, blocks, other, first):
    for i, (ref, top) in enumerate(blocks):
        cols = slice(256 * i, 256 * i + 256)
        xr[cols, :] = ref[top : top + 256, :] * jnp.bfloat16(0.0625)
        ct[0:128, cols] = ref[top + 256 : top + 384, :]
        ct[128:256, cols] = other[128 * (first + i) : 128 * (first + i) + 128, :]


def add_column(xr, ct, x_c, d_c, p_ref, cols, chunk):
    total = jnp.zeros((256, 256), F32)
    start, stop = cols
    for r in range(start, stop, chunk):
        rows = slice(r, r + chunk)
        inner = lax.dot_general(xr[rows, :], x_c, NT, preferred_element_type=F32) + 1.0
        tile = (inner * inner).astype(BF16)
        p_ref[:, rows] += lax.dot_general(d_c, tile, NT, preferred_element_type=F32)
        total += jnp.dot(ct[:, rows], tile, preferred_element_type=F32)
    return total


def columns(refs, other):
    return [
        (ref[0:256, :], jnp.concatenate([ref[256:384, :], other[128 * j : 128 * j + 128, :]]))
        for j, ref in enumerate(refs)
    ]


def kernel_a(*refs):
    z = refs[0:5]
    p0, q0, f, b, other, p_ref, g_ref, xr, ct = refs[5:]
    load_rows(xr, ct, ((p0, 0), (q0, 0), (f, 0), (f, 384), (b, 0), (b, 384)), other, 5)
    p_ref[...] = jnp.zeros_like(p_ref)
    for j, (x_c, d_c) in enumerate(columns(z, other)):
        g_ref[j] = add_column(xr, ct, x_c, d_c, p_ref, (0, 1536), 768)


def kernel_b(f3, b3, p0, q0, f, b, other, other_a, p_in, p_ref, g_ref, xr, ct):
    load_rows(xr, ct, ((p0, 0), (q0, 0), (f, 0), (f, 384), (b, 0), (b, 384)), other_a, 5)
    p_ref[...] = p_in[...]
    for j, (x_c, d_c) in enumerate(columns((f3, b3), other)):
        g_ref[j] = add_column(xr, ct, x_c, d_c, p_ref, (0, 1536), 768)


def kernel_c(w_ref, *refs):
    z = refs[0:7]
    (f4, b4, p0, q0, f, b, far_p, far_q, other, other_b, other_a, p_in, ga, gb) = refs[7:21]
    pm_ref, pq_ref, gm_ref, gq_ref, grad_ref, xr, ct, acc = refs[21:]
    w = w_ref[0]
    load_rows(xr, ct, ((p0, 0), (q0, 0), (f, 0), (f, 384), (b, 0), (b, 384)), other_a, 5)
    load_rows(
        xr.at[1536:2048, :], ct.at[:, 1536:2048], ((far_p, 0), (far_q, 0)), other, 1
    )
    acc[:, 0:1536] = p_in[...]
    acc[:, 1536:2048] = jnp.zeros((256, 512), F32)

    def emit(j, total):
        gm_ref[j] = total[0:128, :] * w
        gq_ref[j] = total[128:256, :] * w

    for j, (x_c, d_c) in enumerate(columns(z[0:5], other_a) + columns(z[5:7], other_b)):
        past = ga[j] if j < 5 else gb[j - 5]
        emit(j, past + add_column(xr, ct, x_c, d_c, acc, (1536, 2048), 512))
    x_c = jnp.concatenate([f4[...], b4[0:64, :]])
    d_c = jnp.concatenate([b4[64:192, :], other[0:128, :]])
    emit(7, add_column(xr, ct, x_c, d_c, acc, (0, 2048), 1024))
    grad = jnp.zeros((256, 256), F32)
    for i in range(8):
        cols = slice(256 * i, 256 * i + 256)
        part = acc[:, cols] * w
        pm_ref[i] = part[0:128, :]
        pq_ref[i] = part[128:256, :]
        grad += part * ct[:, cols].astype(F32)
    grad_ref[...] = jnp.sum(grad.reshape(32, 8, 2, 128), axis=(0, 2))


def call(kernel, name, ins, outs, rows, scratch=(), weight=None):
    vmem = pl.BlockSpec(memory_space=pltpu.VMEM)
    head = () if weight is None else (weight,)
    return pl.pallas_call(
        kernel,
        out_shape=tuple(jax.ShapeDtypeStruct(s, F32) for s in outs),
        in_specs=[pl.BlockSpec(memory_space=pltpu.SMEM)] * len(head) + [vmem] * len(ins),
        out_specs=(vmem,) * len(outs),
        scratch_shapes=[
            pltpu.VMEM((rows, 256), BF16),
            pltpu.VMEM((256, rows), BF16),
            *scratch,
        ],
        compiler_params=pltpu.CompilerParams(vmem_limit_bytes=32 * 1024 * 1024),
        name=name,
    )(*head, *ins)


def voxel_chunk(array, chunk):
    return lax.dynamic_slice_in_dim(array, chunk * 64, 64, 0)


def body(features, direction, cotangent, residual, band_logw, ridge):
    total = features.shape[0] * 64
    weight = jnp.exp(band_logw) * (1.0 / math.sqrt(total))
    yl = lax.axis_index("yl")
    core = lax.axis_index("core")
    own = 2 * yl + core
    also = 2 * (1 - yl) + core
    dir_t, cot_t = direction.T, cotangent.T
    dir_half = jnp.concatenate([voxel_chunk(dir_t, own), voxel_chunk(dir_t, also)])
    cot_half = jnp.concatenate([voxel_chunk(cot_t, own), voxel_chunk(cot_t, also)])
    z0 = jnp.concatenate([features, dir_half])
    p0 = jnp.concatenate([features, cot_half, dir_half])

    f1, b1 = send(z0, "z", 1), send(z0, "z", -1)
    q0 = send(p0, "yh", 1)
    two = jnp.concatenate([p0[0:384], q0[0:384]])
    f2, b2 = send(f1, "z", 1), send(b1, "z", -1)
    pf, pb = send(two, "x", 1), send(two, "x", -1)
    f3, b3 = send(f2, "z", 1), send(b2, "z", -1)
    f4, b4 = send(f3[0:192], "z", 1), send(b3[192:384], "z", -1)
    far_p, far_q = send(pf[0:384], "x", 1), send(pb[384:768], "x", -1)
    z = (z0, f1, b1, f2, b2, f3, b3)
    other_a = send(
        jnp.concatenate(
            [v[256:384] for v in z[0:5]]
            + [p0[256:384], q0[256:384]]
            + [v[s : s + 128] for v in (pf, pb) for s in (256, 640)]
        ),
        "core",
        1,
    )
    other_b = send(jnp.concatenate([f3[256:384], b3[256:384]]), "core", 1)
    other_c = send(jnp.concatenate([b4[64:192], far_p[256:384], far_q[256:384]]), "core", 1)

    rows = (p0, q0, pf, pb)
    p_a, g_a = call(
        kernel_a, "tiles_a", (*z[0:5], *rows, other_a), ((256, 1536), (5, 256, 256)), 1536
    )
    p_b, g_b = call(
        kernel_b,
        "tiles_b",
        (f3, b3, *rows, other_b, other_a, p_a),
        ((256, 1536), (2, 256, 256)),
        1536,
    )
    half = (8, 128, 256)
    p_mine, p_other, g_mine, g_other, grad = call(
        kernel_c,
        "tiles_c",
        (*z, f4, b4, *rows, far_p, far_q, other_c, other_b, other_a, p_b, g_a, g_b),
        (half, half, half, half, (8, 128)),
        2048,
        (pltpu.VMEM((256, 2048), F32),),
        weight,
    )
    p_core = send(p_other, "core", 1)
    g_core = send(g_other, "core", 1)

    ps = [p_mine[i] + p_core[i] for i in range(8)]
    far_f, far_b = send(ps[6], "x", 1), send(ps[7], "x", -1)
    near_f = send(jnp.concatenate([ps[4] + far_f, ps[5]]), "x", 1)
    near_b = send(jnp.concatenate([ps[2], ps[3] + far_b]), "x", -1)
    here = ps[0] + near_f[0:128] + near_b[0:128]
    across = ps[1] + near_f[128:256] + near_b[128:256]
    curve = jnp.sum(
        here * dir_half.astype(F32) + across * q0[384:512].astype(F32), axis=1
    )
    here = here + send(across, "yh", 1)
    product = here[0:64] + send(here[64:128], "yl", 1)

    gs = [g_mine[i] + g_core[i] for i in range(8)]
    gf, gr = send(gs[7][0:64], "z", 1), send(gs[7][64:128], "z", -1)
    gf = send(jnp.concatenate([gs[6][0:64] + gf, gs[6][64:128]]), "z", 1)
    gr = send(jnp.concatenate([gs[5][0:64], gs[5][64:128] + gr]), "z", -1)
    gf, gr = send(gs[4] + gf, "z", 1), send(gs[3] + gr, "z", -1)
    gf, gr = send(gs[2] + gf, "z", 1), send(gs[1] + gr, "z", -1)
    adj = gs[0] + gf + gr
    adj = adj[0:64] + send(adj[64:128], "yl", 1)
    adjoint = adj + ridge[0] * cot_half[0:64].astype(F32)

    dir_own = dir_half[0:64].astype(F32)
    res_t = residual.T
    squares = jnp.sum(res_t * res_t, axis=1)
    curve_own = curve[0:64] + send(curve.reshape(1, 128), "yl", 1)[0, 64:128]
    curve_own = curve_own + ridge[0] * jnp.sum(dir_own * dir_own, axis=1)
    sums = jnp.concatenate([squares, curve_own, jnp.sum(grad, axis=0)]).reshape(1, 256)
    for axis, step in (("x", 1), ("x", 2), ("yh", 1), ("z", 1), ("z", 2), ("z", 4)):
        sums = sums + send(sums, axis, step)
    ratio = sums[0, 0:64] / sums[0, 64:128]
    product = product + ridge[0] * dir_own
    residual_next = res_t - ratio[:, None] * product
    return (residual_next.T, adjoint.T, jnp.sum(sums[0, 128:256]).reshape(1))


def solution(mesh):
    parts = Mesh(mesh.devices.reshape(tuple(SIZES.values())), tuple(SIZES))
    placed = (P(SAMP, BAND), P(SAMP), P(SAMP), P(SAMP, BAND), P(BAND), P())
    return jax.shard_map(
        body,
        mesh=parts,
        in_specs=placed,
        out_specs=(P(SAMP, BAND), P(SAMP, BAND), P(BAND)),
        check_vma=False,
    )
```

```python
import math

import jax
import jax.numpy as jnp
from jax import lax
from jax.experimental import pallas as pl
from jax.experimental.pallas import tpu as pltpu
from jax.sharding import Mesh, PartitionSpec as P

SIZES = {"z": 8, "yh": 2, "x": 4, "yl": 2, "core": 2}
SAMP = ("z", "yh", "x")
BAND = ("yl", "core")
F32 = jnp.float32
BF16 = jnp.bfloat16
NT = (((1,), (1,)), ((), ()))
ZD = (0, 7, 1, 6, 2, 5, 3, 4)
PD = ((0, 0), (1, 0), (0, 3), (1, 3), (0, 1), (1, 1), (0, 2), (1, 2))


def send(value, axis, step):
    n = SIZES[axis]
    return lax.ppermute(value, axis, [(i, (i + step) % n) for i in range(n)])


def swap(chunks, axes):
    return jnp.sum(lax.all_to_all(chunks, axes, 0, 0), axis=0)


def load_rows(xr, ct, blocks, other, first):
    for i, (ref, top) in enumerate(blocks):
        cols = slice(256 * i, 256 * i + 256)
        xr[cols, :] = ref[top : top + 256, :] * jnp.bfloat16(0.0625)
        ct[0:128, cols] = ref[top + 256 : top + 384, :]
        ct[128:256, cols] = other[128 * (first + i) : 128 * (first + i) + 128, :]


def add_column(xr, ct, x_c, d_c, p_ref, cols, chunk):
    total = jnp.zeros((256, 256), F32)
    start, stop = cols
    for r in range(start, stop, chunk):
        rows = slice(r, r + chunk)
        inner = lax.dot_general(xr[rows, :], x_c, NT, preferred_element_type=F32) + 1.0
        tile = (inner * inner).astype(BF16)
        p_ref[:, rows] += lax.dot_general(d_c, tile, NT, preferred_element_type=F32)
        total += jnp.dot(ct[:, rows], tile, preferred_element_type=F32)
    return total


def columns(refs, other):
    return [
        (ref[0:256, :], jnp.concatenate([ref[256:384, :], other[128 * j : 128 * j + 128, :]]))
        for j, ref in enumerate(refs)
    ]


def kernel_a(*refs):
    z = refs[0:5]
    p0, q0, f, b, other, p_ref, g_ref, xr, ct = refs[5:]
    load_rows(xr, ct, ((p0, 0), (q0, 0), (f, 0), (f, 384), (b, 0), (b, 384)), other, 5)
    p_ref[...] = jnp.zeros_like(p_ref)
    for j, (x_c, d_c) in enumerate(columns(z, other)):
        g_ref[j] = add_column(xr, ct, x_c, d_c, p_ref, (0, 1536), 768)


def kernel_b(f3, b3, p0, q0, f, b, other, other_a, p_in, p_ref, g_ref, xr, ct):
    load_rows(xr, ct, ((p0, 0), (q0, 0), (f, 0), (f, 384), (b, 0), (b, 384)), other_a, 5)
    p_ref[...] = p_in[...]
    for j, (x_c, d_c) in enumerate(columns((f3, b3), other)):
        g_ref[j] = add_column(xr, ct, x_c, d_c, p_ref, (0, 1536), 768)


def kernel_c(w_ref, pos_ref, *refs):
    z = refs[0:7]
    (f4, b4, p0, q0, f, b, far_p, far_q, other, other_b, other_a, p_in, ga, gb) = refs[7:21]
    pm_ref, pq_ref, gm_ref, gq_ref, grad_ref, xr, ct, acc = refs[21:]
    w = w_ref[0]
    z_at, yh_at, x_at, yl_at = (pos_ref[i] for i in range(4))
    load_rows(xr, ct, ((p0, 0), (q0, 0), (f, 0), (f, 384), (b, 0), (b, 384)), other_a, 5)
    load_rows(
        xr.at[1536:2048, :], ct.at[:, 1536:2048], ((far_p, 0), (far_q, 0)), other, 1
    )
    acc[:, 0:1536] = p_in[...]
    acc[:, 1536:2048] = jnp.zeros((256, 512), F32)

    def emit(mine, theirs, slot, block):
        mine[2 * slot + yl_at] = block[0:64, :]
        mine[2 * slot + 1 - yl_at] = block[64:128, :]
        theirs[2 * slot + yl_at] = block[128:192, :]
        theirs[2 * slot + 1 - yl_at] = block[192:256, :]

    for j, (x_c, d_c) in enumerate(columns(z[0:5], other_a) + columns(z[5:7], other_b)):
        past = ga[j] if j < 5 else gb[j - 5]
        block = past + add_column(xr, ct, x_c, d_c, acc, (1536, 2048), 512)
        emit(gm_ref, gq_ref, lax.rem(z_at + ZD[j], 8), block * w)
    x_c = jnp.concatenate([f4[...], b4[0:64, :]])
    d_c = jnp.concatenate([b4[64:192, :], other[0:128, :]])
    block = add_column(xr, ct, x_c, d_c, acc, (0, 2048), 1024)
    emit(gm_ref, gq_ref, lax.rem(z_at + ZD[7], 8), block * w)
    grad = jnp.zeros((256, 256), F32)
    for i, (dy, dx) in enumerate(PD):
        cols = slice(256 * i, 256 * i + 256)
        part = acc[:, cols] * w
        emit(pm_ref, pq_ref, 4 * lax.rem(yh_at + dy, 2) + lax.rem(x_at + dx, 4), part)
        grad += part * ct[:, cols].astype(F32)
    grad_ref[...] = jnp.sum(grad.reshape(32, 8, 2, 128), axis=(0, 2))


def call(kernel, name, ins, outs, rows, scratch=(), head=()):
    vmem = pl.BlockSpec(memory_space=pltpu.VMEM)
    return pl.pallas_call(
        kernel,
        out_shape=tuple(jax.ShapeDtypeStruct(s, F32) for s in outs),
        in_specs=[pl.BlockSpec(memory_space=pltpu.SMEM)] * len(head) + [vmem] * len(ins),
        out_specs=(vmem,) * len(outs),
        scratch_shapes=[
            pltpu.VMEM((rows, 256), BF16),
            pltpu.VMEM((256, rows), BF16),
            *scratch,
        ],
        compiler_params=pltpu.CompilerParams(vmem_limit_bytes=32 * 1024 * 1024),
        name=name,
    )(*head, *ins)


def voxel_chunk(array, chunk):
    return lax.dynamic_slice_in_dim(array, chunk * 64, 64, 0)


def body(features, direction, cotangent, residual, band_logw, ridge):
    total = features.shape[0] * 64
    weight = jnp.exp(band_logw) * (1.0 / math.sqrt(total))
    yl = lax.axis_index("yl")
    core = lax.axis_index("core")
    own = 2 * yl + core
    also = 2 * (1 - yl) + core
    dir_t, cot_t = direction.T, cotangent.T
    dir_half = jnp.concatenate([voxel_chunk(dir_t, own), voxel_chunk(dir_t, also)])
    cot_half = jnp.concatenate([voxel_chunk(cot_t, own), voxel_chunk(cot_t, also)])
    z0 = jnp.concatenate([features, dir_half])
    p0 = jnp.concatenate([features, cot_half])

    f1, b1 = send(z0, "z", 1), send(z0, "z", -1)
    q0 = send(p0, "yh", 1)
    f1, b1, q0 = lax.optimization_barrier((f1, b1, q0))
    two = jnp.concatenate([p0, q0])
    pf, pb = send(two, "x", 1), send(two, "x", -1)
    f2, b2 = send(f1, "z", 1), send(b1, "z", -1)
    f3, b3 = send(f2, "z", 1), send(b2, "z", -1)
    far_p, far_q = send(pf[0:384], "x", 1), send(pb[384:768], "x", -1)
    z = (z0, f1, b1, f2, b2, f3, b3)
    other_a = send(
        jnp.concatenate(
            [v[256:384] for v in z[0:5]]
            + [p0[256:384], q0[256:384]]
            + [v[s : s + 128] for v in (pf, pb) for s in (256, 640)]
        ),
        "core",
        1,
    )
    rows = (p0, q0, pf, pb)
    p_a, g_a = call(
        kernel_a, "tiles_a", (*z[0:5], *rows, other_a), ((256, 1536), (5, 256, 256)), 1536
    )
    f3, b3, p_a = lax.optimization_barrier((f3, b3, p_a))
    z = (*z[0:5], f3, b3)
    f4, b4 = send(f3[0:192], "z", 1), send(b3[192:384], "z", -1)
    f4, b4, far_p, far_q = lax.optimization_barrier((f4, b4, far_p, far_q))
    other_b = send(jnp.concatenate([f3[256:384], b3[256:384]]), "core", 1)
    other_c = send(jnp.concatenate([b4[64:192], far_p[256:384], far_q[256:384]]), "core", 1)
    p_b, g_b = call(
        kernel_b,
        "tiles_b",
        (f3, b3, *rows, other_b, other_a, p_a),
        ((256, 1536), (2, 256, 256)),
        1536,
    )
    place = jnp.stack([lax.axis_index(a) for a in ("z", "yh", "x", "yl")]).astype(jnp.int32)
    chunks = (16, 64, 256)
    p_mine, p_other, g_mine, g_other, grad = call(
        kernel_c,
        "tiles_c",
        (*z, f4, b4, *rows, far_p, far_q, other_c, other_b, other_a, p_b, g_a, g_b),
        (chunks, chunks, chunks, chunks, (8, 128)),
        2048,
        (pltpu.VMEM((256, 2048), F32),),
        (weight, place),
    )

    p_sum = p_mine + send(p_other, "core", 1)
    g_sum = g_mine + send(g_other, "core", 1)
    dir_own = dir_half[0:64].astype(F32)
    product = swap(p_sum, ("yh", "x", "yl")) + ridge[0] * dir_own

    res_t = residual.T
    squares = jnp.sum(res_t * res_t, axis=1)
    curve = jnp.sum(dir_own * product, axis=1)
    sums = jnp.concatenate([squares, curve, jnp.sum(grad, axis=0)]).reshape(1, 1, 256)
    same = (lax.broadcasted_iota(jnp.int32, (16, 1, 256), 0) % 2) == yl
    adj = swap(jnp.concatenate([g_sum, jnp.where(same, sums, 0.0)], axis=1), ("z", "yl"))
    adjoint = adj[0:64] + ridge[0] * cot_half[0:64].astype(F32)
    sums = swap(jnp.broadcast_to(adj[64:65], (8, 1, 256)), ("yh", "x"))
    ratio = sums[0, 0:64] / sums[0, 64:128]
    residual_next = res_t - ratio[:, None] * product
    return (residual_next.T, adjoint.T, jnp.sum(sums[0, 128:256]).reshape(1))


def solution(mesh):
    parts = Mesh(mesh.devices.reshape(tuple(SIZES.values())), tuple(SIZES))
    placed = (P(SAMP, BAND), P(SAMP), P(SAMP), P(SAMP, BAND), P(BAND), P())
    return jax.shard_map(
        body,
        mesh=parts,
        in_specs=placed,
        out_specs=(P(SAMP, BAND), P(SAMP, BAND), P(BAND)),
        check_vma=False,
    )
```

```python
import math

import jax
import jax.numpy as jnp
from jax import lax
from jax.experimental import pallas as pl
from jax.experimental.pallas import tpu as pltpu
from jax.sharding import Mesh, PartitionSpec as P

SIZES = {"z": 8, "yh": 2, "x": 4, "yl": 2, "core": 2}
SAMP = ("z", "yh", "x")
BAND = ("yl", "core")
F32 = jnp.float32
BF16 = jnp.bfloat16
NT = (((1,), (1,)), ((), ()))
ZD = (0, 7, 1, 6, 2, 5, 3, 4)
PD = ((0, 0), (1, 0), (0, 3), (1, 3), (0, 1), (1, 1), (0, 2), (1, 2))


def send(value, axis, step):
    n = SIZES[axis]
    return lax.ppermute(value, axis, [(i, (i + step) % n) for i in range(n)])


def swap(chunks, axes):
    return jnp.sum(lax.all_to_all(chunks, axes, 0, 0), axis=0)


def load_rows(xr, ct, first, blocks):
    for i, (ref, top, other, at) in enumerate(blocks, first):
        cols = slice(256 * i, 256 * i + 256)
        xr[cols, :] = ref[top : top + 256, :] * jnp.bfloat16(0.0625)
        ct[0:128, cols] = ref[top + 256 : top + 384, :]
        ct[128:256, cols] = other[at : at + 128, :]


def near_rows(p0, q0, f, b, other):
    blocks = ((p0, 0), (q0, 0), (f, 0), (f, 384), (b, 0), (b, 384))
    return [(ref, top, other, 640 + 128 * i) for i, (ref, top) in enumerate(blocks)]


def far_rows(far_p, far_q, other):
    return [(far_p, 0, other, 256), (far_q, 0, other, 384)]


def add_column(xr, ct, x_c, d_c, p_ref, cols, chunk):
    total = jnp.zeros((256, 256), F32)
    start, stop = cols
    for r in range(start, stop, chunk):
        rows = slice(r, r + chunk)
        inner = lax.dot_general(xr[rows, :], x_c, NT, preferred_element_type=F32) + 1.0
        tile = (inner * inner).astype(BF16)
        p_ref[:, rows] += lax.dot_general(d_c, tile, NT, preferred_element_type=F32)
        total += jnp.dot(ct[:, rows], tile, preferred_element_type=F32)
    return total


def columns(refs, other):
    return [
        (ref[0:256, :], jnp.concatenate([ref[256:384, :], other[128 * j : 128 * j + 128, :]]))
        for j, ref in enumerate(refs)
    ]


def kernel_a(*refs):
    z = refs[0:5]
    p0, q0, f, b, other, p_ref, g_ref, xr, ct = refs[5:]
    load_rows(xr, ct, 0, near_rows(p0, q0, f, b, other))
    p_ref[...] = jnp.zeros_like(p_ref)
    for j, (x_c, d_c) in enumerate(columns(z, other)):
        g_ref[j] = add_column(xr, ct, x_c, d_c, p_ref, (0, 1536), 768)


def kernel_b(w_ref, pos_ref, *refs):
    z = refs[0:7]
    f4, b4, p0, q0, f, b, far_p, far_q, other_a, other_b, p_in, ga = refs[7:19]
    pm_ref, pq_ref, gm_ref, gq_ref, grad_ref, xr, ct, acc = refs[19:]
    w = w_ref[0]
    z_at, yh_at, x_at, yl_at = (pos_ref[i] for i in range(4))
    load_rows(xr, ct, 0, near_rows(p0, q0, f, b, other_a))
    load_rows(xr, ct, 6, far_rows(far_p, far_q, other_b))
    acc[:, 0:1536] = p_in[...]
    acc[:, 1536:2048] = jnp.zeros((256, 512), F32)

    def emit(mine, theirs, slot, block):
        mine[2 * slot + yl_at] = block[0:64, :]
        mine[2 * slot + 1 - yl_at] = block[64:128, :]
        theirs[2 * slot + yl_at] = block[128:192, :]
        theirs[2 * slot + 1 - yl_at] = block[192:256, :]

    late = columns(z[5:7], other_b)
    late.append(
        (
            jnp.concatenate([f4[...], b4[0:64, :]]),
            jnp.concatenate([b4[64:192, :], other_b[512:640, :]]),
        )
    )
    for j, (x_c, d_c) in enumerate(columns(z[0:5], other_a)):
        block = ga[j] + add_column(xr, ct, x_c, d_c, acc, (1536, 2048), 512)
        emit(gm_ref, gq_ref, lax.rem(z_at + ZD[j], 8), block * w)
    for j, (x_c, d_c) in enumerate(late, 5):
        block = add_column(xr, ct, x_c, d_c, acc, (0, 2048), 1024)
        emit(gm_ref, gq_ref, lax.rem(z_at + ZD[j], 8), block * w)
    grad = jnp.zeros((256, 256), F32)
    for i, (dy, dx) in enumerate(PD):
        cols = slice(256 * i, 256 * i + 256)
        part = acc[:, cols] * w
        emit(pm_ref, pq_ref, 4 * lax.rem(yh_at + dy, 2) + lax.rem(x_at + dx, 4), part)
        grad += part * ct[:, cols].astype(F32)
    grad_ref[...] = jnp.sum(grad.reshape(32, 8, 2, 128), axis=(0, 2))


def call(kernel, name, ins, outs, rows, scratch=(), head=()):
    vmem = pl.BlockSpec(memory_space=pltpu.VMEM)
    return pl.pallas_call(
        kernel,
        out_shape=tuple(jax.ShapeDtypeStruct(s, F32) for s in outs),
        in_specs=[pl.BlockSpec(memory_space=pltpu.SMEM)] * len(head) + [vmem] * len(ins),
        out_specs=(vmem,) * len(outs),
        scratch_shapes=[
            pltpu.VMEM((rows, 256), BF16),
            pltpu.VMEM((256, rows), BF16),
            *scratch,
        ],
        compiler_params=pltpu.CompilerParams(vmem_limit_bytes=16 * 1024 * 1024),
        name=name,
    )(*head, *ins)


def voxel_chunk(array, chunk):
    return lax.dynamic_slice_in_dim(array, chunk * 64, 64, 0)


def body(features, direction, cotangent, residual, band_logw, ridge):
    total = features.shape[0] * 64
    weight = jnp.exp(band_logw) * (1.0 / math.sqrt(total))
    yl = lax.axis_index("yl")
    core = lax.axis_index("core")
    own = 2 * yl + core
    also = 2 * (1 - yl) + core
    dir_t, cot_t = direction.T, cotangent.T
    dir_half = jnp.concatenate([voxel_chunk(dir_t, own), voxel_chunk(dir_t, also)])
    cot_half = jnp.concatenate([voxel_chunk(cot_t, own), voxel_chunk(cot_t, also)])
    z0 = jnp.concatenate([features, dir_half])
    p0 = jnp.concatenate([features, cot_half])

    f1, b1 = send(z0, "z", 1), send(z0, "z", -1)
    q0 = send(p0, "yh", 1)
    f1, b1, q0 = lax.optimization_barrier((f1, b1, q0))
    two = jnp.concatenate([p0, q0])
    pf, pb = send(two, "x", 1), send(two, "x", -1)
    f2, b2 = send(f1, "z", 1), send(b1, "z", -1)
    f3, b3 = send(f2, "z", 1), send(b2, "z", -1)
    far_p, far_q = send(pf[0:384], "x", 1), send(pb[384:768], "x", -1)
    z = (z0, f1, b1, f2, b2, f3, b3)
    other_a = send(
        jnp.concatenate(
            [v[256:384] for v in z[0:5]]
            + [p0[256:384], q0[256:384]]
            + [v[s : s + 128] for v in (pf, pb) for s in (256, 640)]
        ),
        "core",
        1,
    )
    rows = (p0, q0, pf, pb)
    p_a, g_a = call(
        kernel_a, "tiles_a", (*z[0:5], *rows, other_a), ((256, 1536), (5, 256, 256)), 1536
    )
    z = (*z[0:5], f3, b3)
    f4, b4 = send(f3[0:192], "z", 1), send(b3[192:384], "z", -1)
    f4, b4, far_p, far_q = lax.optimization_barrier((f4, b4, far_p, far_q))
    rows = (*rows, far_p, far_q)
    other_b = send(
        jnp.concatenate([v[256:384] for v in (f3, b3, far_p, far_q)] + [b4[64:192]]), "core", 1
    )
    place = jnp.stack([lax.axis_index(a) for a in ("z", "yh", "x", "yl")]).astype(jnp.int32)
    chunks = (16, 64, 256)
    p_mine, p_other, g_mine, g_other, grad = call(
        kernel_b,
        "tiles_b",
        (*z, f4, b4, *rows, other_a, other_b, p_a, g_a),
        (chunks, chunks, chunks, chunks, (8, 128)),
        2048,
        (pltpu.VMEM((256, 2048), F32),),
        (weight, place),
    )

    p_sum = p_mine + send(p_other, "core", 1)
    g_sum = g_mine + send(g_other, "core", 1)
    dir_own = dir_half[0:64].astype(F32)
    product = swap(p_sum, ("yh", "x", "yl")) + ridge[0] * dir_own

    def g_block(offset):
        at = 2 * lax.rem(lax.axis_index("z") + offset, 8)
        pair = lax.dynamic_slice_in_dim(g_sum, at, 2, 0)
        return jnp.where(yl == 0, pair, pair[::-1])

    far = g_block(4)
    gf, gr = send(far[:, 0:32], "z", 1), send(far[:, 32:64], "z", -1)
    gf = g_block(3) + jnp.pad(gf, ((0, 0), (0, 32), (0, 0)))
    gr = g_block(5) + jnp.pad(gr, ((0, 0), (32, 0), (0, 0)))
    gf, gr = send(gf, "z", 1), send(gr, "z", -1)
    gf, gr = send(g_block(2) + gf, "z", 1), send(g_block(6) + gr, "z", -1)
    gf, gr = send(g_block(1) + gf, "z", 1), send(g_block(7) + gr, "z", -1)
    adj = g_block(0) + gf + gr
    adj = adj[0] + send(adj[1], "yl", 1)
    res_t = residual.T
    squares = jnp.sum(res_t * res_t, axis=1)
    curve = jnp.sum(dir_own * product, axis=1)
    sums = jnp.concatenate([squares, curve, jnp.sum(grad, axis=0)]).reshape(1, 1, 256)
    sums = swap(jnp.broadcast_to(sums, (64, 1, 256)), SAMP)
    adjoint = adj + ridge[0] * cot_half[0:64].astype(F32)
    ratio = sums[0, 0:64] / sums[0, 64:128]
    residual_next = res_t - ratio[:, None] * product
    return (residual_next.T, adjoint.T, jnp.sum(sums[0, 128:256]).reshape(1))


def solution(mesh):
    parts = Mesh(mesh.devices.reshape(tuple(SIZES.values())), tuple(SIZES))
    placed = (P(SAMP, BAND), P(SAMP), P(SAMP), P(SAMP, BAND), P(BAND), P())
    return jax.shard_map(
        body,
        mesh=parts,
        in_specs=placed,
        out_specs=(P(SAMP, BAND), P(SAMP, BAND), P(BAND)),
        check_vma=False,
    )
```

```python
import math

import jax
import jax.numpy as jnp
from jax import lax
from jax.experimental import pallas as pl
from jax.experimental.pallas import tpu as pltpu
from jax.sharding import Mesh, PartitionSpec as P

SIZES = {"z": 8, "yh": 2, "x": 4, "yl": 2, "core": 2}
SAMP = ("z", "yh", "x")
BAND = ("yl", "core")
F32 = jnp.float32
BF16 = jnp.bfloat16
NT = (((1,), (1,)), ((), ()))
ZD = (0, 7, 1, 6, 2, 5, 3, 4)
PD = ((0, 0), (1, 0), (0, 3), (1, 3), (0, 1), (1, 1), (0, 2), (1, 2))


def send(value, axis, step):
    n = SIZES[axis]
    return lax.ppermute(value, axis, [(i, (i + step) % n) for i in range(n)])


def swap(chunks, axes):
    return jnp.sum(lax.all_to_all(chunks, axes, 0, 0), axis=0)


def load_rows(xr, ct, blocks):
    for i, ref in enumerate(blocks):
        cols = slice(256 * i, 256 * i + 256)
        xr[cols, :] = ref[0:256, :]
        ct[:, cols] = ref[256:512, :]


def add_column(xr, ct, column, p_in, p_ref):
    x_c, d_c = column
    total = jnp.zeros((256, 256), F32)
    for r in range(0, 2048, 1024):
        rows = slice(r, r + 1024)
        inner = lax.dot_general(xr[rows, :], x_c, NT, preferred_element_type=F32) + 1.0
        tile = (inner * inner).astype(BF16)
        part = lax.dot_general(d_c, tile, NT, preferred_element_type=F32)
        p_ref[:, rows] = part if p_in is None else p_in[:, rows] + part
        total += jnp.dot(ct[:, rows], tile, preferred_element_type=F32)
    return total


def kernel_a(*refs):
    z, rows = refs[0:5], refs[5:13]
    p_ref, g_ref, xr, ct = refs[13:]
    load_rows(xr, ct, rows)
    for j, ref in enumerate(z):
        column = (ref[0:256, :], ref[256:512, :])
        g_ref[j] = add_column(xr, ct, column, p_ref if j else None, p_ref)


def kernel_b(w_ref, pos_ref, *refs):
    f3, b3, f4, b4 = refs[0:4]
    rows, p_in, ga = refs[4:12], refs[12], refs[13]
    pm_ref, pq_ref, gm_ref, gq_ref, grad_ref, xr, ct, acc = refs[14:]
    w = w_ref[0]
    z_at, yh_at, x_at, yl_at = (pos_ref[i] for i in range(4))
    load_rows(xr, ct, rows)

    def emit(mine, theirs, slot, block):
        mine[2 * slot + yl_at] = block[0:64, :]
        mine[2 * slot + 1 - yl_at] = block[64:128, :]
        theirs[2 * slot + yl_at] = block[128:192, :]
        theirs[2 * slot + 1 - yl_at] = block[192:256, :]

    columns = [(ref[0:256, :], ref[256:512, :]) for ref in (f3, b3)] + [(f4[...], b4[...])]
    for j in range(8):
        if j < 5:
            block = ga[j]
        else:
            block = add_column(xr, ct, columns[j - 5], p_in if j == 5 else acc, acc)
        emit(gm_ref, gq_ref, lax.rem(z_at + ZD[j], 8), block * w)
    grad = jnp.zeros((256, 256), F32)
    for i, (dy, dx) in enumerate(PD):
        cols = slice(256 * i, 256 * i + 256)
        part = acc[:, cols] * w
        emit(pm_ref, pq_ref, 4 * lax.rem(yh_at + dy, 2) + lax.rem(x_at + dx, 4), part)
        grad += part * ct[:, cols].astype(F32)
    grad_ref[...] = jnp.sum(grad.reshape(32, 8, 2, 128), axis=(0, 2))


def call(kernel, name, ins, outs, scratch=(), head=()):
    vmem = pl.BlockSpec(memory_space=pltpu.VMEM)
    return pl.pallas_call(
        kernel,
        out_shape=tuple(jax.ShapeDtypeStruct(s, F32) for s in outs),
        in_specs=[pl.BlockSpec(memory_space=pltpu.SMEM)] * len(head) + [vmem] * len(ins),
        out_specs=(vmem,) * len(outs),
        scratch_shapes=[
            pltpu.VMEM((2048, 256), BF16),
            pltpu.VMEM((256, 2048), BF16),
            *scratch,
        ],
        compiler_params=pltpu.CompilerParams(vmem_limit_bytes=16 * 1024 * 1024),
        name=name,
    )(*head, *ins)


def body(features, direction, cotangent, residual, band_logw, ridge):
    total = features.shape[0] * 64
    weight = jnp.exp(band_logw) * (1.0 / math.sqrt(total))
    yl = lax.axis_index("yl")
    core = lax.axis_index("core")

    def voxel_major(array):
        parts = [
            lax.dynamic_slice_in_dim(array, 64 * chunk, 64, 1)
            for chunk in (
                2 * yl + core,
                2 * (1 - yl) + core,
                2 * yl + 1 - core,
                2 * (1 - yl) + 1 - core,
            )
        ]
        return jnp.concatenate(parts, axis=1).T

    dir_t, cot_t = voxel_major(direction), voxel_major(cotangent)
    z0 = jnp.concatenate([features, dir_t])
    p0 = jnp.concatenate([features * jnp.bfloat16(0.0625), cot_t])

    f1, b1 = send(z0, "z", 1), send(z0, "z", -1)
    pf, pb = send(p0, "x", 1), send(p0, "x", -1)
    q0 = send(p0, "yh", 1)
    f1, b1, q0, pf, pb = lax.optimization_barrier((f1, b1, q0, pf, pb))
    f2, b2 = send(f1, "z", 1), send(b1, "z", -1)
    qf, qb = send(q0, "x", 1), send(q0, "x", -1)
    f3, b3 = send(f2, "z", 1), send(b2, "z", -1)
    p2, q2 = send(pf, "x", 1), send(qb, "x", -1)
    rows = (p0, q0, pf, qf, pb, qb, p2, q2)
    p_a, g_a = call(
        kernel_a, "tiles_a", (z0, f1, b1, f2, b2, *rows), ((256, 2048), (5, 256, 256))
    )
    f4, b4 = send(f3[0:256], "z", 1), send(b3[256:512], "z", -1)
    place = jnp.stack([lax.axis_index(a) for a in ("z", "yh", "x", "yl")]).astype(jnp.int32)
    chunks = (16, 64, 256)
    p_mine, p_other, g_mine, g_other, grad = call(
        kernel_b,
        "tiles_b",
        (f3, b3, f4, b4, *rows, p_a, g_a),
        (chunks, chunks, chunks, chunks, (8, 128)),
        (pltpu.VMEM((256, 2048), F32),),
        (weight, place),
    )

    p_sum = p_mine + send(p_other, "core", 1)
    p_sum, g_other = lax.optimization_barrier((p_sum, g_other))
    g_sum = g_mine + send(g_other, "core", 1)
    dir_own = dir_t[0:64].astype(F32)
    p_all = lax.all_to_all(p_sum, ("yh", "x", "yl"), 0, 0)

    def g_block(offset):
        at = 2 * lax.rem(lax.axis_index("z") + offset, 8)
        pair = lax.dynamic_slice_in_dim(g_sum, at, 2, 0)
        return jnp.where(yl == 0, pair, pair[::-1])

    far = g_block(4)
    gf, gr = send(far[:, 0:32], "z", 1), send(far[:, 32:64], "z", -1)
    gf = g_block(3) + jnp.pad(gf, ((0, 0), (0, 32), (0, 0)))
    gr = g_block(5) + jnp.pad(gr, ((0, 0), (32, 0), (0, 0)))
    gf, gr = send(gf, "z", 1), send(gr, "z", -1)
    gf, gr = send(g_block(2) + gf, "z", 1), send(g_block(6) + gr, "z", -1)
    gf, gr = send(g_block(1) + gf, "z", 1), send(g_block(7) + gr, "z", -1)
    adj = g_block(0) + gf + gr
    adj, p_all = lax.optimization_barrier((adj, p_all))
    product = jnp.sum(p_all, axis=0) + ridge[0] * dir_own
    adj = adj[0] + send(adj[1], "yl", 1)
    res_t = residual.T
    squares = jnp.sum(res_t * res_t, axis=1)
    curve = jnp.sum(dir_own * product, axis=1)
    sums = jnp.concatenate([squares, curve, jnp.sum(grad, axis=0)]).reshape(1, 1, 256)
    sums = swap(jnp.broadcast_to(sums, (64, 1, 256)), SAMP)
    adjoint = adj + ridge[0] * cot_t[0:64].astype(F32)
    ratio = sums[0, 0:64] / sums[0, 64:128]
    residual_next = res_t - ratio[:, None] * product
    return (residual_next.T, adjoint.T, jnp.sum(sums[0, 128:256]).reshape(1))


def solution(mesh):
    parts = Mesh(mesh.devices.reshape(tuple(SIZES.values())), tuple(SIZES))
    placed = (P(SAMP, BAND), P(SAMP), P(SAMP), P(SAMP, BAND), P(BAND), P())
    return jax.shard_map(
        body,
        mesh=parts,
        in_specs=placed,
        out_specs=(P(SAMP, BAND), P(SAMP, BAND), P(BAND)),
        check_vma=False,
    )
```

```python
import math

import jax
import jax.numpy as jnp
from jax import lax
from jax.experimental import pallas as pl
from jax.experimental.pallas import tpu as pltpu
from jax.sharding import Mesh, PartitionSpec as P

SIZES = {"z": 8, "yh": 2, "x": 4, "yl": 2, "core": 2}
SAMP = ("z", "yh", "x")
BAND = ("yl", "core")
F32 = jnp.float32
BF16 = jnp.bfloat16
NT = (((1,), (1,)), ((), ()))
ZD = (0, 7, 1, 6, 2, 5, 3, 4)
PD = ((0, 0), (1, 0), (0, 3), (1, 3), (0, 1), (1, 1), (0, 2), (1, 2))


def send(value, axis, step):
    n = SIZES[axis]
    return lax.ppermute(value, axis, [(i, (i + step) % n) for i in range(n)])


def load_rows(xr, ct, blocks):
    for i, ref in enumerate(blocks):
        cols = slice(256 * i, 256 * i + 256)
        xr[cols, :] = ref[0:256, :]
        ct[:, cols] = ref[256:512, :]


def add_column(xr, ct, column, p_in, p_ref):
    x_c, d_c = column
    total = jnp.zeros((256, 256), F32)
    for r in range(0, 2048, 1024):
        rows = slice(r, r + 1024)
        inner = lax.dot_general(xr[rows, :], x_c, NT, preferred_element_type=F32) + 1.0
        tile = (inner * inner).astype(BF16)
        part = lax.dot_general(d_c, tile, NT, preferred_element_type=F32)
        p_ref[:, rows] = part if p_in is None else p_in[:, rows] + part
        total += jnp.dot(ct[:, rows], tile, preferred_element_type=F32)
    return total


def kernel_tiles(w_ref, pos_ref, *refs):
    z, rows = refs[0:9], refs[9:17]
    pm_ref, pq_ref, gm_ref, gq_ref, grad_ref, xr, ct, acc = refs[17:]
    w = w_ref[0]
    z_at, yh_at, x_at, yl_at = (pos_ref[i] for i in range(4))
    load_rows(xr, ct, rows)

    def emit(mine, theirs, slot, block):
        mine[2 * slot + yl_at] = block[0:64, :]
        mine[2 * slot + 1 - yl_at] = block[64:128, :]
        theirs[2 * slot + yl_at] = block[128:192, :]
        theirs[2 * slot + 1 - yl_at] = block[192:256, :]

    columns = [(ref[0:256, :], ref[256:512, :]) for ref in z[0:7]]
    columns.append((z[7][...], z[8][...]))
    for j, column in enumerate(columns):
        block = add_column(xr, ct, column, acc if j else None, acc)
        emit(gm_ref, gq_ref, lax.rem(z_at + ZD[j], 8), block * w)
    grad = jnp.zeros((256, 256), F32)
    for i, (dy, dx) in enumerate(PD):
        cols = slice(256 * i, 256 * i + 256)
        part = acc[:, cols] * w
        emit(pm_ref, pq_ref, 4 * lax.rem(yh_at + dy, 2) + lax.rem(x_at + dx, 4), part)
        grad += part * ct[:, cols].astype(F32)
    grad_ref[...] = jnp.sum(grad.reshape(32, 8, 2, 128), axis=(0, 2))


def kernel_fold(pos_ref, mine, theirs, base, grad, *refs):
    rows, out = refs[0:8], refs[8]
    yh_at, x_at, yl_at = (pos_ref[i] for i in range(1, 4))
    curve = jnp.zeros((128, 256), F32)
    for ref, (dy, dx) in zip(rows, PD):
        slot = 4 * lax.rem(yh_at + dy, 2) + lax.rem(x_at + dx, 4)
        at = (2 * slot + yl_at, 2 * slot + 1 - yl_at)
        blocks = [mine[k] + theirs[k] for k in at]
        for k, block in zip(at, blocks):
            out[k, 0:64, :] = block
        curve += jnp.concatenate(blocks) * ref[512:640, :].astype(F32)
    curve = jnp.sum((curve[:, 0:128] + curve[:, 128:256]).T, axis=0, keepdims=True)
    first = lax.broadcasted_iota(jnp.int32, (8, 128), 0) == 0
    sums = jnp.concatenate([base[...] + jnp.where(first, curve, 0.0), grad[...]], axis=1)
    for k in range(16):
        out[k, 64:72, :] = sums


def call(kernel, name, ins, outs, scratch, head=()):
    vmem = pl.BlockSpec(memory_space=pltpu.VMEM)
    return pl.pallas_call(
        kernel,
        out_shape=tuple(jax.ShapeDtypeStruct(s, F32) for s in outs),
        in_specs=[pl.BlockSpec(memory_space=pltpu.SMEM)] * len(head) + [vmem] * len(ins),
        out_specs=(vmem,) * len(outs),
        scratch_shapes=scratch,
        compiler_params=pltpu.CompilerParams(vmem_limit_bytes=16 * 1024 * 1024),
        name=name,
    )(*head, *ins)


def body(features, direction, cotangent, residual, band_logw, ridge):
    total = features.shape[0] * 64
    weight = jnp.exp(band_logw) * (1.0 / math.sqrt(total))
    yl = lax.axis_index("yl")
    core = lax.axis_index("core")

    def voxel_major(array):
        parts = [
            lax.dynamic_slice_in_dim(array, 64 * chunk, 64, 1)
            for chunk in (
                2 * yl + core,
                2 * (1 - yl) + core,
                2 * yl + 1 - core,
                2 * (1 - yl) + 1 - core,
            )
        ]
        return jnp.concatenate(parts, axis=1).T

    dir_t, cot_t = voxel_major(direction), voxel_major(cotangent)
    z0 = jnp.concatenate([features, dir_t])
    p0 = jnp.concatenate([features * jnp.bfloat16(0.0625), cot_t, dir_t[0:128]])

    f1, b1 = send(z0, "z", 1), send(z0, "z", -1)
    pf, pb = send(p0, "x", 1), send(p0, "x", -1)
    q0 = send(p0, "yh", 1)
    f1, b1, q0, pf, pb = lax.optimization_barrier((f1, b1, q0, pf, pb))
    f2, b2 = send(f1, "z", 1), send(b1, "z", -1)
    qf, qb = send(q0, "x", 1), send(q0, "x", -1)
    f2, b2, qf, qb = lax.optimization_barrier((f2, b2, qf, qb))
    f3, b3 = send(f2, "z", 1), send(b2, "z", -1)
    p2, q2 = send(pf, "x", 1), send(qb, "x", -1)
    rows = (p0, q0, pf, qf, pb, qb, p2, q2)
    f4, b4 = send(f3[0:256], "z", 1), send(b3[256:512], "z", -1)
    place = jnp.stack([lax.axis_index(a) for a in ("z", "yh", "x", "yl")]).astype(jnp.int32)
    chunks = (16, 64, 256)
    p_mine, p_other, g_mine, g_other, grad = call(
        kernel_tiles,
        "tiles",
        (z0, f1, b1, f2, b2, f3, b3, f4, b4, *rows),
        (chunks, chunks, chunks, chunks, (8, 128)),
        (
            pltpu.VMEM((2048, 256), BF16),
            pltpu.VMEM((256, 2048), BF16),
            pltpu.VMEM((256, 2048), F32),
        ),
        (weight, place),
    )

    dir_own = dir_t[0:64].astype(F32)
    res_t = residual.T
    squares = jnp.sum(res_t * res_t, axis=1)
    ridged = ridge[0] * jnp.sum(dir_own * dir_own, axis=1)
    base = jnp.pad(jnp.stack([ridged, squares]), ((0, 6), (0, 64)))
    (p_sum,) = call(
        kernel_fold,
        "fold",
        (p_mine, send(p_other, "core", 1), base, grad, *rows),
        ((16, 72, 256),),
        (),
        (place,),
    )
    p_sum, g_other = lax.optimization_barrier((p_sum, g_other))
    g_sum = g_mine + send(g_other, "core", 1)
    p_all = lax.all_to_all(p_sum, ("yh", "x", "yl"), 0, 0)

    def g_block(offset):
        at = 2 * lax.rem(lax.axis_index("z") + offset, 8)
        pair = lax.dynamic_slice_in_dim(g_sum, at, 2, 0)
        return jnp.where(yl == 0, pair, pair[::-1])

    near = [send(g_block(d), "z", d) for d in (1, 7)]
    p_all, near = lax.optimization_barrier((p_all, near))
    away = [send(g_block(d), "z", d) for d in (4, 3, 5, 2, 6)]

    product = jnp.sum(p_all[:, 0:64], axis=0) + ridge[0] * dir_own
    plane = jnp.sum(p_all[:, 64:72].reshape(8, 2, 8, 256), axis=0)
    same, other = jnp.where(yl == 0, plane, plane[::-1])
    sums = jnp.concatenate(
        [same[1, 0:64], same[0, 0:64] + other[0, 64:128], jnp.sum(same[:, 128:256], axis=0)]
    )
    sums = lax.all_to_all(jnp.broadcast_to(sums.reshape(1, 1, 256), (8, 1, 256)), "z", 0, 0)
    sums, away = lax.optimization_barrier((sums, away))
    sums = jnp.sum(sums, axis=0)
    adj = g_block(0) + sum(near + away)
    adj = adj[0] + send(adj[1], "yl", 1)
    adjoint = adj + ridge[0] * cot_t[0:64].astype(F32)
    ratio = sums[0, 0:64] / sums[0, 64:128]
    residual_next = res_t - ratio[:, None] * product
    return (residual_next.T, adjoint.T, jnp.sum(sums[0, 128:256]).reshape(1))


def solution(mesh):
    parts = Mesh(mesh.devices.reshape(tuple(SIZES.values())), tuple(SIZES))
    placed = (P(SAMP, BAND), P(SAMP), P(SAMP), P(SAMP, BAND), P(BAND), P())
    return jax.shard_map(
        body,
        mesh=parts,
        in_specs=placed,
        out_specs=(P(SAMP, BAND), P(SAMP, BAND), P(BAND)),
        check_vma=False,
    )
```

```python
import math

import jax
import jax.numpy as jnp
from jax import lax
from jax.experimental import pallas as pl
from jax.experimental.pallas import tpu as pltpu
from jax.sharding import Mesh, PartitionSpec as P

SIZES = {"z": 8, "yh": 2, "x": 4, "yl": 2, "core": 2}
SAMP = ("z", "yh", "x")
BAND = ("yl", "core")
F32 = jnp.float32
BF16 = jnp.bfloat16
NT = (((1,), (1,)), ((), ()))
ZD = (0, 7, 1, 6, 2, 5, 3, 4)
PD = ((0, 0), (1, 0), (0, 3), (1, 3), (0, 1), (1, 1), (0, 2), (1, 2))


def send(value, axis, step):
    n = SIZES[axis]
    return lax.ppermute(value, axis, [(i, (i + step) % n) for i in range(n)])


def load_rows(xr, ct, blocks):
    for i, ref in enumerate(blocks):
        cols = slice(256 * i, 256 * i + 256)
        xr[cols, :] = ref[0:256, :]
        ct[:, cols] = ref[256:512, :]


def add_column(xr, ct, column, p_in, p_ref):
    x_c, d_c = column
    total = jnp.zeros((256, 256), F32)
    for r in range(0, 2048, 1024):
        rows = slice(r, r + 1024)
        inner = lax.dot_general(xr[rows, :], x_c, NT, preferred_element_type=F32) + 1.0
        tile = (inner * inner).astype(BF16)
        part = lax.dot_general(d_c, tile, NT, preferred_element_type=F32)
        p_ref[:, rows] = part if p_in is None else p_in[:, rows] + part
        total += jnp.dot(ct[:, rows], tile, preferred_element_type=F32)
    return total


def kernel_tiles(w_ref, pos_ref, *refs):
    z, rows = refs[0:9], refs[9:17]
    pm_ref, pq_ref, gm_ref, gq_ref, grad_ref, xr, ct, acc = refs[17:]
    w = w_ref[0]
    z_at, yh_at, x_at, yl_at = (pos_ref[i] for i in range(4))
    load_rows(xr, ct, rows)

    def emit(mine, theirs, slot, block):
        mine[2 * slot + yl_at] = block[0:64, :]
        mine[2 * slot + 1 - yl_at] = block[64:128, :]
        theirs[2 * slot + yl_at] = block[128:192, :]
        theirs[2 * slot + 1 - yl_at] = block[192:256, :]

    columns = [(ref[0:256, :], ref[256:512, :]) for ref in z[0:7]]
    columns.append((z[7][...], z[8][...]))
    for j, column in enumerate(columns):
        block = add_column(xr, ct, column, acc if j else None, acc)
        emit(gm_ref, gq_ref, lax.rem(z_at + ZD[j], 8), block * w)
    grad = jnp.zeros((256, 256), F32)
    for i, (dy, dx) in enumerate(PD):
        cols = slice(256 * i, 256 * i + 256)
        part = acc[:, cols] * w
        emit(pm_ref, pq_ref, 4 * lax.rem(yh_at + dy, 2) + lax.rem(x_at + dx, 4), part)
        grad += part * ct[:, cols].astype(F32)
    grad_ref[...] = jnp.sum(grad.reshape(32, 8, 2, 128), axis=(0, 2))


def kernel_fold(pos_ref, mine, theirs, base, grad, *refs):
    rows, out = refs[0:8], refs[21]
    yh_at, x_at, yl_at = (pos_ref[i] for i in range(1, 4))
    curve = jnp.zeros((128, 256), F32)
    for ref, (dy, dx) in zip(rows, PD):
        slot = 4 * lax.rem(yh_at + dy, 2) + lax.rem(x_at + dx, 4)
        at = (2 * slot + yl_at, 2 * slot + 1 - yl_at)
        blocks = [mine[k] + theirs[k] for k in at]
        for k, block in zip(at, blocks):
            out[k, 0:64, :] = block
        curve += jnp.concatenate(blocks) * ref[512:640, :].astype(F32)
    curve = jnp.sum((curve[:, 0:128] + curve[:, 128:256]).T, axis=0, keepdims=True)
    first = lax.broadcasted_iota(jnp.int32, (8, 128), 0) == 0
    sums = jnp.concatenate([base[...] + jnp.where(first, curve, 0.0), grad[...]], axis=1)
    for k in range(16):
        out[k, 64:72, :] = sums


def call(kernel, name, ins, outs, scratch, head=()):
    vmem = pl.BlockSpec(memory_space=pltpu.VMEM)
    return pl.pallas_call(
        kernel,
        out_shape=tuple(jax.ShapeDtypeStruct(s, F32) for s in outs),
        in_specs=[pl.BlockSpec(memory_space=pltpu.SMEM)] * len(head) + [vmem] * len(ins),
        out_specs=(vmem,) * len(outs),
        scratch_shapes=scratch,
        compiler_params=pltpu.CompilerParams(vmem_limit_bytes=16 * 1024 * 1024),
        name=name,
    )(*head, *ins)


def body(features, direction, cotangent, residual, band_logw, ridge):
    total = features.shape[0] * 64
    weight = jnp.exp(band_logw) * (1.0 / math.sqrt(total))
    yl = lax.axis_index("yl")
    core = lax.axis_index("core")

    def voxel_major(array):
        parts = [
            lax.dynamic_slice_in_dim(array, 64 * chunk, 64, 1)
            for chunk in (
                2 * yl + core,
                2 * (1 - yl) + core,
                2 * yl + 1 - core,
                2 * (1 - yl) + 1 - core,
            )
        ]
        return jnp.concatenate(parts, axis=1).T

    dir_t, cot_t = voxel_major(direction), voxel_major(cotangent)
    z0 = jnp.concatenate([features, dir_t])
    p0 = jnp.concatenate([features * jnp.bfloat16(0.0625), cot_t, dir_t[0:128]])

    f1, b1 = send(z0, "z", 1), send(z0, "z", -1)
    pf, pb = send(p0, "x", 1), send(p0, "x", -1)
    q0 = send(p0, "yh", 1)
    f1, b1, q0, pf, pb = lax.optimization_barrier((f1, b1, q0, pf, pb))
    f2, b2 = send(f1, "z", 1), send(b1, "z", -1)
    qf, qb = send(q0, "x", 1), send(q0, "x", -1)
    f2, b2, qf, qb = lax.optimization_barrier((f2, b2, qf, qb))
    f3, b3 = send(f2, "z", 1), send(b2, "z", -1)
    p2, q2 = send(pf, "x", 1), send(qb, "x", -1)
    rows = (p0, q0, pf, qf, pb, qb, p2, q2)
    f4, b4 = send(f3[0:256], "z", 1), send(b3[256:512], "z", -1)
    place = jnp.stack([lax.axis_index(a) for a in ("z", "yh", "x", "yl")]).astype(jnp.int32)
    chunks = (16, 64, 256)
    p_mine, p_other, g_mine, g_other, grad = call(
        kernel_tiles,
        "tiles",
        (z0, f1, b1, f2, b2, f3, b3, f4, b4, *rows),
        (chunks, chunks, chunks, chunks, (8, 128)),
        (
            pltpu.VMEM((2048, 256), BF16),
            pltpu.VMEM((256, 2048), BF16),
            pltpu.VMEM((256, 2048), F32),
        ),
        (weight, place),
    )

    dir_own = dir_t[0:64].astype(F32)
    res_t = residual.T
    squares = jnp.sum(res_t * res_t, axis=1)
    ridged = ridge[0] * jnp.sum(dir_own * dir_own, axis=1)
    base = jnp.pad(jnp.stack([ridged, squares]), ((0, 6), (0, 64)))
    (p_sum,) = call(
        kernel_fold,
        "fold",
        (p_mine, send(p_other, "core", 1), base, grad, *rows, z0, f1, b1, f2, b2, f3, b3, f4, b4, f1, b1, f2, b2),
        ((16, 72, 256),),
        (),
        (place,),
    )
    p_sum, g_other = lax.optimization_barrier((p_sum, g_other))
    g_sum = g_mine + send(g_other, "core", 1)
    p_all = lax.all_to_all(p_sum, ("yh", "x", "yl"), 0, 0)

    def g_block(offset):
        at = 2 * lax.rem(lax.axis_index("z") + offset, 8)
        pair = lax.dynamic_slice_in_dim(g_sum, at, 2, 0)
        return jnp.where(yl == 0, pair, pair[::-1])

    near = [send(g_block(d), "z", d) for d in (1, 7)]
    p_all, near = lax.optimization_barrier((p_all, near))
    away = [send(g_block(d), "z", d) for d in (4, 3, 5, 2, 6)]

    product = jnp.sum(p_all[:, 0:64], axis=0) + ridge[0] * dir_own
    plane = jnp.sum(p_all[:, 64:72].reshape(8, 2, 8, 256), axis=0)
    same, other = jnp.where(yl == 0, plane, plane[::-1])
    sums = jnp.concatenate(
        [same[1, 0:64], same[0, 0:64] + other[0, 64:128], jnp.sum(same[:, 128:256], axis=0)]
    )
    sums = lax.all_to_all(jnp.broadcast_to(sums.reshape(1, 1, 256), (8, 1, 256)), "z", 0, 0)
    sums, away = lax.optimization_barrier((sums, away))
    sums = jnp.sum(sums, axis=0)
    adj = g_block(0) + sum(near + away)
    adj = adj[0] + send(adj[1], "yl", 1)
    adjoint = adj + ridge[0] * cot_t[0:64].astype(F32)
    ratio = sums[0, 0:64] / sums[0, 64:128]
    residual_next = res_t - ratio[:, None] * product
    return (residual_next.T, adjoint.T, jnp.sum(sums[0, 128:256]).reshape(1))


def solution(mesh):
    parts = Mesh(mesh.devices.reshape(tuple(SIZES.values())), tuple(SIZES))
    placed = (P(SAMP, BAND), P(SAMP), P(SAMP), P(SAMP, BAND), P(BAND), P())
    return jax.shard_map(
        body,
        mesh=parts,
        in_specs=placed,
        out_specs=(P(SAMP, BAND), P(SAMP, BAND), P(BAND)),
        check_vma=False,
    )
```

```python
import math

import jax
import jax.numpy as jnp
from jax import lax
from jax.experimental import pallas as pl
from jax.experimental.pallas import tpu as pltpu
from jax.sharding import Mesh, PartitionSpec as P

SIZES = {"z": 8, "yh": 2, "x": 4, "yl": 2, "core": 2}
SAMP = ("z", "yh", "x")
BAND = ("yl", "core")
F32 = jnp.float32
BF16 = jnp.bfloat16
NT = (((1,), (1,)), ((), ()))
ZD = (0, 7, 1, 6, 2, 5, 3, 4)
PD = ((0, 0), (1, 0), (0, 3), (1, 3), (0, 1), (1, 1), (0, 2), (1, 2))


def send(value, axis, step):
    n = SIZES[axis]
    return lax.ppermute(value, axis, [(i, (i + step) % n) for i in range(n)])


def load_rows(xr, ct, blocks):
    for i, ref in enumerate(blocks):
        cols = slice(256 * i, 256 * i + 256)
        xr[cols, :] = ref[0:256, :]
        ct[:, cols] = ref[256:512, :]


def add_column(xr, ct, column, p_in, p_ref):
    x_c, d_c = column
    total = jnp.zeros((256, 256), F32)
    for r in range(0, 2048, 1024):
        rows = slice(r, r + 1024)
        inner = lax.dot_general(xr[rows, :], x_c, NT, preferred_element_type=F32) + 1.0
        tile = (inner * inner).astype(BF16)
        part = lax.dot_general(d_c, tile, NT, preferred_element_type=F32)
        p_ref[:, rows] = part if p_in is None else p_in[:, rows] + part
        total += jnp.dot(ct[:, rows], tile, preferred_element_type=F32)
    return total


def kernel_a(*refs):
    z, rows = refs[0:5], refs[5:13]
    p_ref, g_ref, xr, ct = refs[13:]
    load_rows(xr, ct, rows)
    for j, ref in enumerate(z):
        column = (ref[0:256, :], ref[256:512, :])
        g_ref[j] = add_column(xr, ct, column, p_ref if j else None, p_ref)


def kernel_b(w_ref, pos_ref, *refs):
    f3, b3, f4, b4 = refs[0:4]
    rows, p_in, ga = refs[4:12], refs[12], refs[13]
    pm_ref, pq_ref, gm_ref, gq_ref, grad_ref, xr, ct, acc = refs[14:]
    w = w_ref[0]
    z_at, yh_at, x_at, yl_at = (pos_ref[i] for i in range(4))
    load_rows(xr, ct, rows)

    def emit(mine, theirs, slot, block):
        mine[2 * slot + yl_at] = block[0:64, :]
        mine[2 * slot + 1 - yl_at] = block[64:128, :]
        theirs[2 * slot + yl_at] = block[128:192, :]
        theirs[2 * slot + 1 - yl_at] = block[192:256, :]

    columns = [(ref[0:256, :], ref[256:512, :]) for ref in (f3, b3)] + [(f4[...], b4[...])]
    for j in range(8):
        if j < 5:
            block = ga[j]
        else:
            block = add_column(xr, ct, columns[j - 5], p_in if j == 5 else acc, acc)
        emit(gm_ref, gq_ref, lax.rem(z_at + ZD[j], 8), block * w)
    grad = jnp.zeros((256, 256), F32)
    for i, (dy, dx) in enumerate(PD):
        cols = slice(256 * i, 256 * i + 256)
        part = acc[:, cols] * w
        emit(pm_ref, pq_ref, 4 * lax.rem(yh_at + dy, 2) + lax.rem(x_at + dx, 4), part)
        grad += part * ct[:, cols].astype(F32)
    grad_ref[...] = jnp.sum(grad.reshape(32, 8, 2, 128), axis=(0, 2))


def kernel_fold(pos_ref, mine, theirs, base, grad, *refs):
    rows, out = refs[0:8], refs[32]
    yh_at, x_at, yl_at = (pos_ref[i] for i in range(1, 4))
    curve = jnp.zeros((128, 256), F32)
    for ref, (dy, dx) in zip(rows, PD):
        slot = 4 * lax.rem(yh_at + dy, 2) + lax.rem(x_at + dx, 4)
        at = (2 * slot + yl_at, 2 * slot + 1 - yl_at)
        blocks = [mine[k] + theirs[k] for k in at]
        for k, block in zip(at, blocks):
            out[k, 0:64, :] = block
        curve += jnp.concatenate(blocks) * ref[512:640, :].astype(F32)
    curve = jnp.sum((curve[:, 0:128] + curve[:, 128:256]).T, axis=0, keepdims=True)
    first = lax.broadcasted_iota(jnp.int32, (8, 128), 0) == 0
    sums = jnp.concatenate([base[...] + jnp.where(first, curve, 0.0), grad[...]], axis=1)
    for k in range(16):
        out[k, 64:72, :] = sums


def call(kernel, name, ins, outs, scratch, head=()):
    vmem = pl.BlockSpec(memory_space=pltpu.VMEM)
    return pl.pallas_call(
        kernel,
        out_shape=tuple(jax.ShapeDtypeStruct(s, F32) for s in outs),
        in_specs=[pl.BlockSpec(memory_space=pltpu.SMEM)] * len(head) + [vmem] * len(ins),
        out_specs=(vmem,) * len(outs),
        scratch_shapes=scratch,
        compiler_params=pltpu.CompilerParams(vmem_limit_bytes=16 * 1024 * 1024),
        name=name,
    )(*head, *ins)


def body(features, direction, cotangent, residual, band_logw, ridge):
    total = features.shape[0] * 64
    weight = jnp.exp(band_logw) * (1.0 / math.sqrt(total))
    yl = lax.axis_index("yl")
    core = lax.axis_index("core")

    def voxel_major(array):
        parts = [
            lax.dynamic_slice_in_dim(array, 64 * chunk, 64, 1)
            for chunk in (
                2 * yl + core,
                2 * (1 - yl) + core,
                2 * yl + 1 - core,
                2 * (1 - yl) + 1 - core,
            )
        ]
        return jnp.concatenate(parts, axis=1).T

    dir_t, cot_t = voxel_major(direction), voxel_major(cotangent)
    z0 = jnp.concatenate([features, dir_t])
    p0 = jnp.concatenate([features * jnp.bfloat16(0.0625), cot_t, dir_t[0:128]])

    f1, b1 = send(z0, "z", 1), send(z0, "z", -1)
    pf, pb = send(p0, "x", 1), send(p0, "x", -1)
    q0 = send(p0, "yh", 1)
    f1, b1, q0, pf, pb = lax.optimization_barrier((f1, b1, q0, pf, pb))
    f2, b2 = send(f1, "z", 1), send(b1, "z", -1)
    qf, qb = send(q0, "x", 1), send(q0, "x", -1)
    f2, b2, qf, qb = lax.optimization_barrier((f2, b2, qf, qb))
    f3, b3 = send(f2, "z", 1), send(b2, "z", -1)
    p2, q2 = send(pf, "x", 1), send(qb, "x", -1)
    rows = (p0, q0, pf, qf, pb, qb, p2, q2)
    f4, b4 = send(f3[0:256], "z", 1), send(b3[256:512], "z", -1)
    place = jnp.stack([lax.axis_index(a) for a in ("z", "yh", "x", "yl")]).astype(jnp.int32)
    chunks = (16, 64, 256)
    tiles = (pltpu.VMEM((2048, 256), BF16), pltpu.VMEM((256, 2048), BF16))
    p_a, g_a = call(
        kernel_a, "tiles_a", (z0, f1, b1, f2, b2, *rows), ((256, 2048), (5, 256, 256)), tiles
    )
    p_mine, p_other, g_mine, g_other, grad = call(
        kernel_b,
        "tiles_b",
        (f3, b3, f4, b4, *rows, p_a, g_a),
        (chunks, chunks, chunks, chunks, (8, 128)),
        (*tiles, pltpu.VMEM((256, 2048), F32)),
        (weight, place),
    )

    dir_own = dir_t[0:64].astype(F32)
    res_t = residual.T
    squares = jnp.sum(res_t * res_t, axis=1)
    ridged = ridge[0] * jnp.sum(dir_own * dir_own, axis=1)
    base = jnp.pad(jnp.stack([ridged, squares]), ((0, 6), (0, 64)))
    (p_sum,) = call(
        kernel_fold,
        "fold",
        (p_mine, send(p_other, "core", 1), base, grad, *rows, z0, f1, b1, f2, b2, f3, b3, f4, b4, f1, b1, f2, b2, f3, b3, f1, b1, f2, b2, f3, b3, z0, f4, b4),
        ((16, 72, 256),),
        (),
        (place,),
    )
    p_sum, g_other = lax.optimization_barrier((p_sum, g_other))
    g_sum = g_mine + send(g_other, "core", 1)
    p_all = lax.all_to_all(p_sum, ("yh", "x", "yl"), 0, 0)

    def g_block(offset):
        at = 2 * lax.rem(lax.axis_index("z") + offset, 8)
        pair = lax.dynamic_slice_in_dim(g_sum, at, 2, 0)
        return jnp.where(yl == 0, pair, pair[::-1])

    near = [send(g_block(d), "z", d) for d in (1, 7)]
    p_all, near = lax.optimization_barrier((p_all, near))
    away = [send(g_block(d), "z", d) for d in (4, 3, 5, 2, 6)]

    product = jnp.sum(p_all[:, 0:64], axis=0) + ridge[0] * dir_own
    plane = jnp.sum(p_all[:, 64:72].reshape(8, 2, 8, 256), axis=0)
    same, other = jnp.where(yl == 0, plane, plane[::-1])
    sums = jnp.concatenate(
        [same[1, 0:64], same[0, 0:64] + other[0, 64:128], jnp.sum(same[:, 128:256], axis=0)]
    )
    sums = lax.all_to_all(jnp.broadcast_to(sums.reshape(1, 1, 256), (8, 1, 256)), "z", 0, 0)
    sums, away = lax.optimization_barrier((sums, away))
    sums = jnp.sum(sums, axis=0)
    adj = g_block(0) + sum(near + away)
    adj = adj[0] + send(adj[1], "yl", 1)
    adjoint = adj + ridge[0] * cot_t[0:64].astype(F32)
    ratio = sums[0, 0:64] / sums[0, 64:128]
    residual_next = res_t - ratio[:, None] * product
    return (residual_next.T, adjoint.T, jnp.sum(sums[0, 128:256]).reshape(1))


def solution(mesh):
    parts = Mesh(mesh.devices.reshape(tuple(SIZES.values())), tuple(SIZES))
    placed = (P(SAMP, BAND), P(SAMP), P(SAMP), P(SAMP, BAND), P(BAND), P())
    return jax.shard_map(
        body,
        mesh=parts,
        in_specs=placed,
        out_specs=(P(SAMP, BAND), P(SAMP, BAND), P(BAND)),
        check_vma=False,
    )
```

```python
import math

import jax
import jax.numpy as jnp
from jax import lax
from jax.experimental import pallas as pl
from jax.experimental.pallas import tpu as pltpu
from jax.sharding import Mesh, PartitionSpec as P

SIZES = {"z": 8, "yh": 2, "x": 4, "yl": 2, "core": 2}
SAMP = ("z", "yh", "x")
BAND = ("yl", "core")
F32 = jnp.float32
BF16 = jnp.bfloat16
NT = (((1,), (1,)), ((), ()))
ZD = (0, 7, 1, 6, 2, 5, 3, 4)
PD = ((0, 0), (1, 0), (0, 3), (1, 3), (0, 1), (1, 1), (0, 2), (1, 2))


def send(value, axis, step):
    n = SIZES[axis]
    return lax.ppermute(value, axis, [(i, (i + step) % n) for i in range(n)])


def load_rows(xr, ct, blocks):
    for i, ref in enumerate(blocks):
        cols = slice(256 * i, 256 * i + 256)
        xr[cols, :] = ref[0:256, :]
        ct[:, cols] = ref[256:512, :]


def add_column(xr, ct, column, p_in, p_ref):
    x_c, d_c = column
    total = jnp.zeros((256, 256), F32)
    for r in range(0, 2048, 1024):
        rows = slice(r, r + 1024)
        inner = lax.dot_general(xr[rows, :], x_c, NT, preferred_element_type=F32) + 1.0
        tile = (inner * inner).astype(BF16)
        part = lax.dot_general(d_c, tile, NT, preferred_element_type=F32)
        p_ref[:, rows] = part if p_in is None else p_in[:, rows] + part
        total += jnp.dot(ct[:, rows], tile, preferred_element_type=F32)
    return total


def kernel_a(*refs):
    z, rows = refs[0:5], refs[5:13]
    p_ref, g_ref, xr, ct = refs[13:]
    load_rows(xr, ct, rows)
    for j, ref in enumerate(z):
        column = (ref[0:256, :], ref[256:512, :])
        g_ref[j] = add_column(xr, ct, column, p_ref if j else None, p_ref)


def kernel_b(w_ref, pos_ref, *refs):
    f3, b3, f4, b4 = refs[0:4]
    rows, p_in, ga = refs[4:12], refs[12], refs[13]
    pm_ref, pq_ref, gm_ref, gq_ref, grad_ref, xr, ct, acc = refs[14:]
    w = w_ref[0]
    z_at, yh_at, x_at, yl_at = (pos_ref[i] for i in range(4))
    load_rows(xr, ct, rows)

    def emit(mine, theirs, slot, block):
        mine[2 * slot + yl_at] = block[0:64, :]
        mine[2 * slot + 1 - yl_at] = block[64:128, :]
        theirs[2 * slot + yl_at] = block[128:192, :]
        theirs[2 * slot + 1 - yl_at] = block[192:256, :]

    columns = [(ref[0:256, :], ref[256:512, :]) for ref in (f3, b3)] + [(f4[...], b4[...])]
    for j in range(8):
        if j < 5:
            block = ga[j]
        else:
            block = add_column(xr, ct, columns[j - 5], p_in if j == 5 else acc, acc)
        emit(gm_ref, gq_ref, lax.rem(z_at + ZD[j], 8), block * w)
    grad = jnp.zeros((256, 256), F32)
    for i, (dy, dx) in enumerate(PD):
        cols = slice(256 * i, 256 * i + 256)
        part = acc[:, cols] * w
        emit(pm_ref, pq_ref, 4 * lax.rem(yh_at + dy, 2) + lax.rem(x_at + dx, 4), part)
        grad += part * ct[:, cols].astype(F32)
    grad_ref[...] = jnp.sum(grad.reshape(32, 8, 2, 128), axis=(0, 2))


def kernel_fold(pos_ref, mine, theirs, base, grad, *refs):
    rows, out = refs[0:8], refs[32]
    yh_at, x_at, yl_at = (pos_ref[i] for i in range(1, 4))
    curve = jnp.zeros((128, 256), F32)
    for ref, (dy, dx) in zip(rows, PD):
        slot = 4 * lax.rem(yh_at + dy, 2) + lax.rem(x_at + dx, 4)
        at = (2 * slot + yl_at, 2 * slot + 1 - yl_at)
        blocks = [mine[k] + theirs[k] for k in at]
        for k, block in zip(at, blocks):
            out[k, 0:64, :] = block
        curve += jnp.concatenate(blocks) * ref[512:640, :].astype(F32)
    curve = jnp.sum((curve[:, 0:128] + curve[:, 128:256]).T, axis=0, keepdims=True)
    first = lax.broadcasted_iota(jnp.int32, (8, 128), 0) == 0
    sums = jnp.concatenate([base[...] + jnp.where(first, curve, 0.0), grad[...]], axis=1)
    for k in range(16):
        out[k, 64:72, :] = sums


def call(kernel, name, ins, outs, scratch, head=()):
    vmem = pl.BlockSpec(memory_space=pltpu.VMEM)
    return pl.pallas_call(
        kernel,
        out_shape=tuple(jax.ShapeDtypeStruct(s, F32) for s in outs),
        in_specs=[pl.BlockSpec(memory_space=pltpu.SMEM)] * len(head) + [vmem] * len(ins),
        out_specs=(vmem,) * len(outs),
        scratch_shapes=scratch,
        compiler_params=pltpu.CompilerParams(vmem_limit_bytes=16 * 1024 * 1024),
        name=name,
    )(*head, *ins)


def body(features, direction, cotangent, residual, band_logw, ridge):
    total = features.shape[0] * 64
    weight = jnp.exp(band_logw) * (1.0 / math.sqrt(total))
    yl = lax.axis_index("yl")
    core = lax.axis_index("core")

    def voxel_major(array):
        parts = [
            lax.dynamic_slice_in_dim(array, 64 * chunk, 64, 1)
            for chunk in (
                2 * yl + core,
                2 * (1 - yl) + core,
                2 * yl + 1 - core,
                2 * (1 - yl) + 1 - core,
            )
        ]
        return jnp.concatenate(parts, axis=1).T

    dir_t, cot_t = voxel_major(direction), voxel_major(cotangent)
    z0 = jnp.concatenate([features, dir_t])
    p0 = jnp.concatenate([features * jnp.bfloat16(0.0625), cot_t, dir_t[0:128]])

    f1, b1 = send(z0, "z", 1), send(z0, "z", -1)
    pf, pb = send(p0, "x", 1), send(p0, "x", -1)
    q0 = send(p0, "yh", 1)
    q0, pf, pb = lax.optimization_barrier((q0, pf, pb))
    f2, b2 = send(f1, "z", 1), send(b1, "z", -1)
    qf, qb = send(q0, "x", 1), send(q0, "x", -1)
    f2, b2, qf, qb = lax.optimization_barrier((f2, b2, qf, qb))
    f3, b3 = send(f2, "z", 1), send(b2, "z", -1)
    p2, q2 = send(pf, "x", 1), send(qb, "x", -1)
    rows = (p0, q0, pf, qf, pb, qb, p2, q2)
    f4, b4 = send(f3[0:256], "z", 1), send(b3[256:512], "z", -1)
    place = jnp.stack([lax.axis_index(a) for a in ("z", "yh", "x", "yl")]).astype(jnp.int32)
    chunks = (16, 64, 256)
    tiles = (pltpu.VMEM((2048, 256), BF16), pltpu.VMEM((256, 2048), BF16))
    p_a, g_a = call(
        kernel_a, "tiles_a", (z0, f1, b1, f2, b2, *rows), ((256, 2048), (5, 256, 256)), tiles
    )
    p_mine, p_other, g_mine, g_other, grad = call(
        kernel_b,
        "tiles_b",
        (f3, b3, f4, b4, *rows, p_a, g_a),
        (chunks, chunks, chunks, chunks, (8, 128)),
        (*tiles, pltpu.VMEM((256, 2048), F32)),
        (weight, place),
    )

    dir_own = dir_t[0:64].astype(F32)
    res_t = residual.T
    squares = jnp.sum(res_t * res_t, axis=1)
    ridged = ridge[0] * jnp.sum(dir_own * dir_own, axis=1)
    base = jnp.pad(jnp.stack([ridged, squares]), ((0, 6), (0, 64)))
    (p_sum,) = call(
        kernel_fold,
        "fold",
        (p_mine, send(p_other, "core", 1), base, grad, *rows, z0, f1, b1, f2, b2, f3, b3, f4, b4, f1, b1, f2, b2, f3, b3, f1, b1, f2, b2, f3, b3, z0, f4, b4),
        ((16, 72, 256),),
        (),
        (place,),
    )
    p_sum, g_other = lax.optimization_barrier((p_sum, g_other))
    g_sum = g_mine + send(g_other, "core", 1)
    p_all = lax.all_to_all(p_sum, ("yh", "x", "yl"), 0, 0)

    def g_block(offset):
        at = 2 * lax.rem(lax.axis_index("z") + offset, 8)
        pair = lax.dynamic_slice_in_dim(g_sum, at, 2, 0)
        return jnp.where(yl == 0, pair, pair[::-1])

    near = [send(g_block(d), "z", d) for d in (1, 7)]
    p_all, near = lax.optimization_barrier((p_all, near))
    away = [send(g_block(d), "z", d) for d in (4, 3, 5, 2, 6)]

    product = jnp.sum(p_all[:, 0:64], axis=0) + ridge[0] * dir_own
    plane = jnp.sum(p_all[:, 64:72].reshape(8, 2, 8, 256), axis=0)
    same, other = jnp.where(yl == 0, plane, plane[::-1])
    sums = jnp.concatenate(
        [same[1, 0:64], same[0, 0:64] + other[0, 64:128], jnp.sum(same[:, 128:256], axis=0)]
    )
    sums = lax.all_to_all(jnp.broadcast_to(sums.reshape(1, 1, 256), (8, 1, 256)), "z", 0, 0)
    sums, away = lax.optimization_barrier((sums, away))
    sums = jnp.sum(sums, axis=0)
    adj = g_block(0) + sum(near + away)
    adj = adj[0] + send(adj[1], "yl", 1)
    adjoint = adj + ridge[0] * cot_t[0:64].astype(F32)
    ratio = sums[0, 0:64] / sums[0, 64:128]
    residual_next = res_t - ratio[:, None] * product
    return (residual_next.T, adjoint.T, jnp.sum(sums[0, 128:256]).reshape(1))


def solution(mesh):
    parts = Mesh(mesh.devices.reshape(tuple(SIZES.values())), tuple(SIZES))
    placed = (P(SAMP, BAND), P(SAMP), P(SAMP), P(SAMP, BAND), P(BAND), P())
    return jax.shard_map(
        body,
        mesh=parts,
        in_specs=placed,
        out_specs=(P(SAMP, BAND), P(SAMP, BAND), P(BAND)),
        check_vma=False,
    )
```

```python
import math

import jax
import jax.numpy as jnp
from jax import lax
from jax.experimental import pallas as pl
from jax.experimental.pallas import tpu as pltpu
from jax.sharding import Mesh, PartitionSpec as P

SIZES = {"z": 8, "yh": 2, "x": 4, "yl": 2, "core": 2}
SAMP = ("z", "yh", "x")
BAND = ("yl", "core")
F32 = jnp.float32
BF16 = jnp.bfloat16
NT = (((1,), (1,)), ((), ()))
ZD = (0, 7, 1, 6, 2, 5, 3, 4)
PD = ((0, 0), (1, 0), (0, 3), (1, 3), (0, 1), (1, 1), (0, 2), (1, 2))


def send(value, axis, step):
    n = SIZES[axis]
    return lax.ppermute(value, axis, [(i, (i + step) % n) for i in range(n)])


def load_rows(xr, ct, blocks):
    for i, ref in enumerate(blocks):
        cols = slice(256 * i, 256 * i + 256)
        xr[cols, :] = ref[0:256, :]
        ct[:, cols] = ref[256:512, :]


def add_column(xr, ct, column, p_in, p_ref):
    x_c, d_c = column
    total = jnp.zeros((256, 256), F32)
    for r in range(0, 2048, 1024):
        rows = slice(r, r + 1024)
        inner = lax.dot_general(xr[rows, :], x_c, NT, preferred_element_type=F32) + 1.0
        tile = (inner * inner).astype(BF16)
        part = lax.dot_general(d_c, tile, NT, preferred_element_type=F32)
        p_ref[:, rows] = part if p_in is None else p_in[:, rows] + part
        total += jnp.dot(ct[:, rows], tile, preferred_element_type=F32)
    return total


def kernel_a(*refs):
    z, rows = refs[0:5], refs[5:13]
    p_ref, g_ref, xr, ct = refs[13:]
    load_rows(xr, ct, rows)
    for j, ref in enumerate(z):
        column = (ref[0:256, :], ref[256:512, :])
        g_ref[j] = add_column(xr, ct, column, p_ref if j else None, p_ref)


def kernel_b(w_ref, pos_ref, *refs):
    f3, b3, f4, b4 = refs[0:4]
    rows, p_in, ga = refs[4:12], refs[12], refs[13]
    pm_ref, pq_ref, gm_ref, gq_ref, grad_ref, xr, ct, acc = refs[14:]
    w = w_ref[0]
    z_at, yh_at, x_at, yl_at = (pos_ref[i] for i in range(4))
    load_rows(xr, ct, rows)

    def emit(mine, theirs, slot, block):
        mine[2 * slot + yl_at] = block[0:64, :]
        mine[2 * slot + 1 - yl_at] = block[64:128, :]
        theirs[2 * slot + yl_at] = block[128:192, :]
        theirs[2 * slot + 1 - yl_at] = block[192:256, :]

    columns = [(ref[0:256, :], ref[256:512, :]) for ref in (f3, b3)] + [(f4[...], b4[...])]
    for j in range(8):
        if j < 5:
            block = ga[j]
        else:
            block = add_column(xr, ct, columns[j - 5], p_in if j == 5 else acc, acc)
        emit(gm_ref, gq_ref, lax.rem(z_at + ZD[j], 8), block * w)
    grad = jnp.zeros((256, 256), F32)
    for i, (dy, dx) in enumerate(PD):
        cols = slice(256 * i, 256 * i + 256)
        part = acc[:, cols] * w
        emit(pm_ref, pq_ref, 4 * lax.rem(yh_at + dy, 2) + lax.rem(x_at + dx, 4), part)
        grad += part * ct[:, cols].astype(F32)
    grad_ref[...] = jnp.sum(grad.reshape(32, 8, 2, 128), axis=(0, 2))


def kernel_fold(pos_ref, mine, theirs, base, grad, *refs):
    rows, out = refs[0:8], refs[32]
    yh_at, x_at, yl_at = (pos_ref[i] for i in range(1, 4))
    curve = jnp.zeros((128, 256), F32)
    for ref, (dy, dx) in zip(rows, PD):
        slot = 4 * lax.rem(yh_at + dy, 2) + lax.rem(x_at + dx, 4)
        at = (2 * slot + yl_at, 2 * slot + 1 - yl_at)
        blocks = [mine[k] + theirs[k] for k in at]
        for k, block in zip(at, blocks):
            out[k, 0:64, :] = block
        curve += jnp.concatenate(blocks) * ref[512:640, :].astype(F32)
    curve = jnp.sum((curve[:, 0:128] + curve[:, 128:256]).T, axis=0, keepdims=True)
    first = lax.broadcasted_iota(jnp.int32, (8, 128), 0) == 0
    sums = jnp.concatenate([base[...] + jnp.where(first, curve, 0.0), grad[...]], axis=1)
    for k in range(16):
        out[k, 64:72, :] = sums


def call(kernel, name, ins, outs, scratch, head=()):
    vmem = pl.BlockSpec(memory_space=pltpu.VMEM)
    return pl.pallas_call(
        kernel,
        out_shape=tuple(jax.ShapeDtypeStruct(s, F32) for s in outs),
        in_specs=[pl.BlockSpec(memory_space=pltpu.SMEM)] * len(head) + [vmem] * len(ins),
        out_specs=(vmem,) * len(outs),
        scratch_shapes=scratch,
        compiler_params=pltpu.CompilerParams(vmem_limit_bytes=16 * 1024 * 1024),
        name=name,
    )(*head, *ins)


def body(features, direction, cotangent, residual, band_logw, ridge):
    total = features.shape[0] * 64
    weight = jnp.exp(band_logw) * (1.0 / math.sqrt(total))
    yl = lax.axis_index("yl")
    core = lax.axis_index("core")

    def voxel_major(array):
        parts = [
            lax.dynamic_slice_in_dim(array, 64 * chunk, 64, 1)
            for chunk in (
                2 * yl + core,
                2 * (1 - yl) + core,
                2 * yl + 1 - core,
                2 * (1 - yl) + 1 - core,
            )
        ]
        return jnp.concatenate(parts, axis=1).T

    dir_t, cot_t = voxel_major(direction), voxel_major(cotangent)
    z0 = jnp.concatenate([features, dir_t])
    p0 = jnp.concatenate([features * jnp.bfloat16(0.0625), cot_t, dir_t[0:128]])

    f1, b1 = send(z0, "z", 1), send(z0, "z", -1)
    pf, pb = send(p0, "x", 1), send(p0, "x", -1)
    q0 = send(p0, "yh", 1)
    q0, pf, pb = lax.optimization_barrier((q0, pf, pb))
    f2, b2 = send(f1, "z", 1), send(b1, "z", -1)
    qf, qb = send(q0, "x", 1), send(q0, "x", -1)
    qf, qb, pf = lax.optimization_barrier((qf, qb, pf))
    f3, b3 = send(f2, "z", 1), send(b2, "z", -1)
    p2, q2 = send(pf, "x", 1), send(qb, "x", -1)
    rows = (p0, q0, pf, qf, pb, qb, p2, q2)
    f4, b4 = send(f3[0:256], "z", 1), send(b3[256:512], "z", -1)
    place = jnp.stack([lax.axis_index(a) for a in ("z", "yh", "x", "yl")]).astype(jnp.int32)
    chunks = (16, 64, 256)
    tiles = (pltpu.VMEM((2048, 256), BF16), pltpu.VMEM((256, 2048), BF16))
    p_a, g_a = call(
        kernel_a, "tiles_a", (z0, f1, b1, f2, b2, *rows), ((256, 2048), (5, 256, 256)), tiles
    )
    p_mine, p_other, g_mine, g_other, grad = call(
        kernel_b,
        "tiles_b",
        (f3, b3, f4, b4, *rows, p_a, g_a),
        (chunks, chunks, chunks, chunks, (8, 128)),
        (*tiles, pltpu.VMEM((256, 2048), F32)),
        (weight, place),
    )

    dir_own = dir_t[0:64].astype(F32)
    res_t = residual.T
    squares = jnp.sum(res_t * res_t, axis=1)
    ridged = ridge[0] * jnp.sum(dir_own * dir_own, axis=1)
    base = jnp.pad(jnp.stack([ridged, squares]), ((0, 6), (0, 64)))
    (p_sum,) = call(
        kernel_fold,
        "fold",
        (p_mine, send(p_other, "core", 1), base, grad, *rows, z0, f1, b1, f2, b2, f3, b3, f4, b4, f1, b1, f2, b2, f3, b3, f1, b1, f2, b2, f3, b3, z0, f4, b4),
        ((16, 72, 256),),
        (),
        (place,),
    )
    p_sum, g_other = lax.optimization_barrier((p_sum, g_other))
    g_sum = g_mine + send(g_other, "core", 1)
    p_all = lax.all_to_all(p_sum, ("yh", "x", "yl"), 0, 0)

    def g_block(offset):
        at = 2 * lax.rem(lax.axis_index("z") + offset, 8)
        pair = lax.dynamic_slice_in_dim(g_sum, at, 2, 0)
        return jnp.where(yl == 0, pair, pair[::-1])

    near = [send(g_block(d), "z", d) for d in (1, 7)]
    p_all, near = lax.optimization_barrier((p_all, near))
    away = [send(g_block(d), "z", d) for d in (4, 3, 5, 2, 6)]

    product = jnp.sum(p_all[:, 0:64], axis=0) + ridge[0] * dir_own
    plane = jnp.sum(p_all[:, 64:72].reshape(8, 2, 8, 256), axis=0)
    same, other = jnp.where(yl == 0, plane, plane[::-1])
    sums = jnp.concatenate(
        [same[1, 0:64], same[0, 0:64] + other[0, 64:128], jnp.sum(same[:, 128:256], axis=0)]
    )
    sums = lax.all_to_all(jnp.broadcast_to(sums.reshape(1, 1, 256), (8, 1, 256)), "z", 0, 0)
    sums, away = lax.optimization_barrier((sums, away))
    sums = jnp.sum(sums, axis=0)
    adj = g_block(0) + sum(near + away)
    adj = adj[0] + send(adj[1], "yl", 1)
    adjoint = adj + ridge[0] * cot_t[0:64].astype(F32)
    ratio = sums[0, 0:64] / sums[0, 64:128]
    residual_next = res_t - ratio[:, None] * product
    return (residual_next.T, adjoint.T, jnp.sum(sums[0, 128:256]).reshape(1))


def solution(mesh):
    parts = Mesh(mesh.devices.reshape(tuple(SIZES.values())), tuple(SIZES))
    placed = (P(SAMP, BAND), P(SAMP), P(SAMP), P(SAMP, BAND), P(BAND), P())
    return jax.shard_map(
        body,
        mesh=parts,
        in_specs=placed,
        out_specs=(P(SAMP, BAND), P(SAMP, BAND), P(BAND)),
        check_vma=False,
    )
```
